32 devices in a mesh: dp: 8 (over z, y), graph: 4 (over x, core).
Axes of the slice: x: 2, y: 2, z: 4, core: 2. Of those that a mesh axis runs over, the one named last changes fastest.
Arguments:
- atoms: bfloat16 [8, 4, 1024, 128], P('dp', 'graph'), may hold values from -80 to 80, as said below
- gain: float32 [128], replicated, may hold values from 0.1 to 1.9
- w_src: bfloat16 [128, 128], replicated, may hold values from -0.5 to 0.5
- w_edge: bfloat16 [128, 128], replicated, may hold values from -0.5 to 0.5
- w_out: bfloat16 [128, 128], replicated, may hold values from -0.5 to 0.5
- send_src: int32 [8, 4, 4, 2048], P('dp', 'graph'), may hold values from 0 to 1023
- recv_dst: int32 [8, 4, 4, 2048], P('dp', 'graph'), may hold values from 0 to 1023
- edge_count: int32 [8, 4, 4], P('dp'), may hold values from 512 to 2048, as said below
- edge_feat: bfloat16 [8, 4, 4, 2048, 128], P('dp', 'graph'), may hold values from -6 to 6
- cotangent: bfloat16 [8, 4, 1024, 128], P('dp', 'graph'), may hold values from -6 to 6
Outputs:
- layer_out: bfloat16 [8, 4, 1024, 128], P('dp', 'graph')
- grad_atoms: bfloat16 [8, 4, 1024, 128], P('dp', 'graph')
- grad_w_src: float32 [128, 128], P('dp')
- grad_w_edge: float32 [128, 128], P('dp')
- grad_w_out: float32 [128, 128], P('dp')
- grad_gain: float32 [128], P('dp')
The draws below stay inside these ranges and needn't reach their ends.
Inputs may be any that keep to these rules, and one draw needn't show every extreme that they name: `atoms`: row scales of the atom features vary. `edge_count`: every batch has one destination shard that receives more; in every draw some shard sends exactly 2048 live slots to some shard.
All inputs are finite; a program needn't handle non-finite values.
Results may differ from the reference program's by a relative error of at most 0.0059.
Values may be sent and summed in bfloat16 or wider, within the bound.
No kernel may reach another device: no remote copies, remote signals or barrier semaphores. Data moves between devices by JAX's collectives and lax.ppermute only.
A program may use at most 64 MiB of HBM per device.

```python
import math
import jax
import jax.numpy as jnp
from jax import lax

C = 128
H = 128
EDGE = 128
A_DEV = 1024
CAP = 2048
DEG_NORM = 23
N_DP = 8
N_GRAPH = 4


def draw_atoms(key, part):
    first, second = jax.random.split(jax.random.fold_in(key, 5), 2)
    shape = (N_DP, N_GRAPH, A_DEV, C)
    base = jax.random.normal(first, shape, jnp.float32)
    scales = jnp.exp(jax.random.uniform(second, (N_DP, N_GRAPH, A_DEV, 1), jnp.float32, 0.0, math.log(10.0)))
    values = base * scales
    return jnp.clip(values, -80.0, 80.0).astype(jnp.bfloat16)


def draw_edge_count(key, part):
    keys = jax.random.split(jax.random.fold_in(key, 3), 5)
    base = jax.random.randint(keys[0], (N_DP, N_GRAPH, N_GRAPH), CAP // 4, CAP // 2 + 1)
    hot = jax.random.randint(keys[1], (N_DP, 1, 1), 0, N_GRAPH)
    extra = jax.random.randint(keys[2], (N_DP, N_GRAPH, N_GRAPH), 0, CAP // 2)
    target = jnp.arange(N_GRAPH, dtype=jnp.int32)[None, None, :]
    counts = base + jnp.where(target == hot, extra, 0)
    row_pick = jax.random.randint(keys[3], (), 0, N_GRAPH)
    col_pick = jax.random.randint(keys[4], (), 0, N_GRAPH)
    counts = counts.at[:, row_pick, col_pick].set(CAP)
    return counts.astype(jnp.int32)


def place_ends(entries, own_key, least, top_value):
    place = [jax.random.randint(jax.random.fold_in(own_key, axis), (), 0, length) for axis, length in enumerate(entries.shape)]
    longest = entries.shape.index(max(entries.shape))
    next_to = place[:longest] + [(place[longest] + 1) % entries.shape[longest]] + place[longest + 1:]
    return entries.at[tuple(place)].set(least).at[tuple(next_to)].set(top_value)


def steps_of(key, shape, cuts, least, largest):
    def one(position, shards_of):
        heights = jax.random.uniform(jax.random.fold_in(jax.random.fold_in(key, 6), position), (shards_of,), jnp.float32, least / len(cuts), largest / len(cuts))
        return jnp.repeat(jnp.exp(heights), shape[position] // shards_of).reshape((-1,) + (1,) * (len(shape) - position - 1))

    loudness = one(*cuts[0])
    for cut in cuts[1:]:
        loudness = loudness * one(*cut)
    return loudness


def noise(key, shape, scale, bound, pieces=(), kind=jnp.bfloat16):
    values = scale * jax.random.normal(key, shape, jnp.float32)
    if pieces:
        values = values * steps_of(key, shape, pieces, -0.22, 0.18)
    return jnp.clip(values, -bound, bound).astype(kind)


def setup_inputs(seed: int = 0) -> dict:
    arg_keys = jax.random.split(jax.random.key(seed), 11)
    return {
        "atoms": draw_atoms(jax.random.fold_in(arg_keys[10], 71), 0),
        "gain": jnp.clip(1.0 + 0.18 * jax.random.normal(arg_keys[1], (C,), jnp.float32), 0.1, 1.9),
        "w_src": noise(arg_keys[2], (C, H), C ** -0.5, 0.5),
        "w_edge": noise(arg_keys[3], (EDGE, H), EDGE ** -0.5, 0.5),
        "w_out": noise(arg_keys[4], (H, C), H ** -0.5, 0.5),
        "send_src": place_ends(jax.random.randint(arg_keys[5], (N_DP, N_GRAPH, N_GRAPH, CAP), 0, A_DEV), jax.random.fold_in(arg_keys[5], 1), 0, A_DEV - 1).astype(jnp.int32),
        "recv_dst": place_ends(jax.random.randint(arg_keys[6], (N_DP, N_GRAPH, N_GRAPH, CAP), 0, A_DEV), jax.random.fold_in(arg_keys[6], 1), 0, A_DEV - 1).astype(jnp.int32),
        "edge_count": draw_edge_count(jax.random.fold_in(arg_keys[10], 71), 0),
        "edge_feat": noise(arg_keys[8], (N_DP, N_GRAPH, N_GRAPH, CAP, EDGE), 1.0, 6.0, ((0, 8), (1, 4))),
        "cotangent": noise(arg_keys[9], (N_DP, N_GRAPH, A_DEV, C), 1.0, 6.0, ((0, 8), (1, 4))),
    }


def silu_slope(pre):
    sig = jax.nn.sigmoid(pre)
    return sig * (1.0 + pre * (1.0 - sig))

def reference(atoms, gain, w_src, w_edge, w_out, send_src, recv_dst, edge_count, edge_feat, cotangent):

    def one_batch(inputs):
        feats, srcs, dsts, counts, edges, cot = inputs
        hfull = feats.astype(jnp.float32)
        inv = lax.rsqrt(lax.optimization_barrier(jnp.mean(hfull * hfull, axis=-1)) + 1e-06)
        normed = (hfull * inv[..., None] * gain).astype(jnp.bfloat16).reshape(N_GRAPH * A_DEV, C)
        src_flat = (jnp.arange(N_GRAPH, dtype=jnp.int32)[:, None, None] * A_DEV + srcs).reshape(-1)
        rows = jnp.take(normed, src_flat, axis=0)
        edge_rows = edges.reshape(-1, EDGE)
        pre = jnp.dot(rows, w_src, preferred_element_type=jnp.float32) + jnp.dot(edge_rows, w_edge, preferred_element_type=jnp.float32)
        valid = (jnp.arange(CAP, dtype=jnp.int32)[None, None, :] < counts[:, :, None]).astype(jnp.float32).reshape(-1, 1)
        msg = (jax.nn.silu(pre) * valid).astype(jnp.bfloat16)
        dst_local = jnp.transpose(dsts, (1, 0, 2))
        dst_flat = (jnp.arange(N_GRAPH, dtype=jnp.int32)[None, :, None] * A_DEV + dst_local).reshape(-1)
        agg = (jax.ops.segment_sum(msg.astype(jnp.float32), dst_flat, num_segments=N_GRAPH * A_DEV) / DEG_NORM).astype(jnp.bfloat16)
        out = (hfull.reshape(-1, C) + jnp.dot(agg, w_out, preferred_element_type=jnp.float32)).astype(jnp.bfloat16)
        cot_flat = cot.reshape(-1, C)
        back = (lax.dot_general(cot_flat, w_out, (((1,), (1,)), ((), ())), preferred_element_type=jnp.float32) / DEG_NORM).astype(jnp.bfloat16)
        slot_back = jnp.take(back, dst_flat, axis=0)
        dpre = (slot_back.astype(jnp.float32) * silu_slope(pre) * valid).astype(jnp.bfloat16)
        grad_src = lax.dot_general(rows, dpre, (((0,), (0,)), ((), ())), preferred_element_type=jnp.float32)
        grad_edge = lax.dot_general(edge_rows, dpre, (((0,), (0,)), ((), ())), preferred_element_type=jnp.float32)
        grad_out = lax.dot_general(agg, cot_flat, (((0,), (0,)), ((), ())), preferred_element_type=jnp.float32)
        dnorm_rows = lax.dot_general(dpre, w_src, (((1,), (1,)), ((), ())), preferred_element_type=jnp.float32)
        dnorm = jax.ops.segment_sum(dnorm_rows, src_flat, num_segments=N_GRAPH * A_DEV).reshape(N_GRAPH, A_DEV, C)
        scaled = gain * dnorm
        grad_g = lax.optimization_barrier(jnp.sum(dnorm * hfull * inv[..., None], axis=(0, 1)))
        grad_h = cot.astype(jnp.float32) + inv[..., None] * scaled - hfull * (inv ** 3)[..., None] * lax.optimization_barrier(jnp.mean(hfull * scaled, axis=-1, keepdims=True))
        return (out.reshape(N_GRAPH, A_DEV, C), grad_h.astype(jnp.bfloat16), grad_src, grad_edge, grad_out, grad_g)
    outs = lax.map(one_batch, (atoms, send_src, recv_dst, edge_count, edge_feat, cotangent))
    layer_out, grad_atoms, grad_src, grad_edge, grad_out, grad_g = outs
    return (layer_out, grad_atoms, lax.optimization_barrier(jnp.sum(grad_src, axis=0)), lax.optimization_barrier(jnp.sum(grad_edge, axis=0)), lax.optimization_barrier(jnp.sum(grad_out, axis=0)), lax.optimization_barrier(jnp.sum(grad_g, axis=0)))
```

```python
import functools

import jax
import jax.numpy as jnp
from jax import lax
from jax.experimental import pallas as pl
from jax.experimental.pallas import tpu as pltpu
from jax.sharding import PartitionSpec as P

DEG_NORM = 23
GROUP = 256
BLOCK = 512
F32 = jnp.float32
BF16 = jnp.bfloat16
VMEM_BYTES = 48 * 1024 * 1024


def dot(a, b):
    return jnp.dot(a, b, preferred_element_type=F32)


def dot_nt(a, b):
    return lax.dot_general(a, b, (((1,), (1,)), ((), ())), preferred_element_type=F32)


def split(x):
    high = x.astype(BF16)
    return high, (x - high.astype(F32)).astype(BF16)


def stack_groups(x, groups):
    return jnp.concatenate([x[:, g * GROUP : (g + 1) * GROUP] for g in range(groups)], axis=0)


def unstack_groups(x, groups):
    rows = x.shape[0] // groups
    return jnp.concatenate([x[g * rows : (g + 1) * rows, :] for g in range(groups)], axis=1)


def spread(x, which, groups):
    return jnp.concatenate([x * (which == g).astype(F32).astype(BF16) for g in range(groups)], axis=0)


def choose(x, which, groups):
    rows = x.shape[0] // groups
    out = x[:rows, :]
    for g in range(1, groups):
        out = jnp.where(which == g, x[g * rows : (g + 1) * rows, :], out)
    return out


def one_hot(low):
    place = lax.broadcasted_iota(jnp.int32, (GROUP, low.shape[1]), 0)
    return jnp.where(place == low, 1.0, 0.0).astype(BF16)


def norm_parts(atoms, gain):
    feats = atoms.astype(F32).T
    inv = lax.rsqrt(jnp.mean(feats * feats, axis=0, keepdims=True) + 1e-06)
    return feats, inv


def edge_kernel(
    info,
    atoms,
    gain,
    w_src,
    w_edge,
    w_out,
    src,
    dst,
    edges,
    cot,
    part,
    chunks,
    dnorm_out,
    table,
    back,
    agg_sum,
    src_sum,
    edge_sum,
):
    shards, slots = src.shape
    atom_count, chans = atoms.shape
    groups = atom_count // GROUP
    blocks = slots // BLOCK
    feats, inv = norm_parts(atoms[...], gain)
    normed = (feats * inv * gain[...]).astype(BF16)
    table[...] = stack_groups(normed, groups)
    src_sum[...] = jnp.zeros_like(src_sum)
    edge_sum[...] = jnp.zeros_like(edge_sum)
    w_src_t = w_src[...].T
    w_edge_t = w_edge[...].T
    grad_out = jnp.zeros((w_out.shape[0], chans), F32)
    for k in range(shards):
        peer = info[k]
        count = info[shards + k]
        back_t = (dot_nt(w_out[...], cot[k]) * (1.0 / DEG_NORM)).astype(BF16)
        back[...] = stack_groups(back_t, groups)
        agg_sum[...] = jnp.zeros_like(agg_sum)

        def step(block, carry, k=k, peer=peer, count=count):
            start = pl.multiple_of(block * BLOCK, BLOCK)
            span = pl.ds(start, BLOCK)
            s = src[pl.ds(peer, 1), span]
            d = dst[k : k + 1, span]
            live = lax.broadcasted_iota(jnp.int32, (1, BLOCK), 1) + start < count
            s_low = jnp.where(live, s % GROUP, -1)
            d_low = jnp.where(live, d % GROUP, -1)
            s_high = s // GROUP
            d_high = d // GROUP
            s_hot = one_hot(s_low)
            d_hot = one_hot(d_low)
            e = edges[peer, span, :]
            rows = choose(dot(table[...], s_hot), s_high, groups).astype(BF16)
            pre = dot(w_src_t, rows) + dot_nt(w_edge_t, e)
            sig = 0.5 * jnp.tanh(0.5 * pre) + 0.5
            act = pre * sig
            slope = sig + act - act * sig
            agg_sum[...] += dot_nt(spread(act.astype(BF16), d_high, groups), d_hot)
            slot_back = choose(dot(back[...], d_hot), d_high, groups)
            dpre = (slot_back * slope).astype(BF16)
            edge_sum[...] += dot(dpre, e)
            src_sum[...] += dot_nt(spread(dpre, s_high, groups), s_hot)
            return carry

        lax.fori_loop(0, (count + BLOCK - 1) // BLOCK, step, 0)
        part_k = (unstack_groups(agg_sum[...], groups) * (1.0 / DEG_NORM)).astype(BF16)
        part[k] = part_k
        grad_out = grad_out + dot(part_k, cot[k])
    high, low = split(unstack_groups(src_sum[...], groups))
    grad_src = dot_nt(normed, high) + dot_nt(normed, low)
    dnorm = dot(w_src[...], high) + dot(w_src[...], low)
    dnorm_out[...] = dnorm
    grad_gain = jnp.sum(dnorm * feats * inv, axis=1, keepdims=True)
    grad_gain = jnp.broadcast_to(grad_gain, (chans, chans)).T
    grad_edge = edge_sum[...].T
    batches = chunks.shape[0]
    rows = chans // batches
    mine = info[2 * shards]
    for j in range(batches):
        place = j ^ mine
        for i, grad in enumerate((grad_src, grad_edge, grad_out)):
            chunks[place, i * rows : (i + 1) * rows, :] = grad[j * rows : (j + 1) * rows, :]
        chunks[place, 3 * rows :, :] = grad_gain[: chunks.shape[1] - 3 * rows, :]


def atom_kernel(atoms, gain, w_out, cot, dnorm, agg_a, agg_b, layer_out, grad_atoms):
    feats, inv = norm_parts(atoms[...], gain)
    agg = (agg_a[...].astype(F32) + agg_b[...].astype(F32)).T.astype(BF16)
    layer_out[...] = (atoms[...].astype(F32) + dot(agg, w_out[...])).astype(BF16)
    scaled = gain[...] * dnorm[...]
    mean = jnp.mean(feats * scaled, axis=0, keepdims=True)
    rest = inv * scaled - feats * (inv * inv * inv * mean)
    grad_atoms[...] = (cot[...].astype(F32) + rest.T).astype(BF16)


def move(x, axis, bit):
    size = lax.axis_size(axis)
    return lax.ppermute(x, axis, [(i, i ^ bit) for i in range(size)])


def move_both(x, batch_bit, graph_bit):
    batches, shards = lax.axis_size("dp"), lax.axis_size("graph")
    pairs = [
        (b * shards + g, (b ^ batch_bit) * shards + (g ^ graph_bit))
        for b in range(batches)
        for g in range(shards)
    ]
    return lax.ppermute(x, ("dp", "graph"), pairs)


def reduce_chunks(chunks):
    batches, rows, width = chunks.shape
    total = chunks + move(chunks, "graph", 1)
    pair = total.reshape(batches // 2, 2, rows, width)
    keep, give = pair[:, 0], pair[:, 1]
    total = keep + move(keep, "graph", 2) + move(give, "dp", 1) + move_both(give, 1, 2)
    bit = 2
    while bit < batches:
        left = batches // bit
        fan = min(4, left)
        parts = total.reshape(left // fan, fan, rows, width)
        total = parts[:, 0]
        for k in range(1, fan):
            total = total + move(parts[:, k], "dp", k * bit)
        bit *= fan
    return total.reshape(rows, width)


def body(atoms, gain, w_src, w_edge, w_out, send_src, recv_dst, edge_count, edge_feat, cotangent):
    shards = lax.axis_size("graph")
    batches = lax.axis_size("dp")
    myself = lax.axis_index("graph")
    batch = lax.axis_index("dp")
    atom_count, chans = atoms.shape[2:]
    slots = send_src.shape[3]
    groups = atom_count // GROUP
    feats = atoms.reshape(atom_count, chans)
    src = send_src.reshape(shards, slots)
    dst_here = recv_dst.reshape(shards, slots)
    cot = cotangent.reshape(atom_count, chans)
    gain_col = gain.reshape(chans, 1)
    peers = [myself ^ k for k in range(shards)]

    dst = [lax.dynamic_index_in_dim(dst_here, p, 0, keepdims=False) for p in peers]
    dst = [dst[0]] + [move(dst[k], "graph", k) for k in range(1, shards)]
    far = move(cot, "graph", 2)
    near = move(cot, "graph", 1)
    cots = jnp.stack([cot, near, far, move(far, "graph", 1)])

    sends = lax.dynamic_index_in_dim(edge_count[0], myself, 0, keepdims=False)
    info = jnp.stack(
        peers + [lax.dynamic_index_in_dim(sends, p, 0, keepdims=False) for p in peers] + [batch]
    ).astype(jnp.int32)

    rows = chans // batches
    chunk_rows = -(-(3 * rows + 1) // 8) * 8
    vmem = pl.BlockSpec(memory_space=pltpu.VMEM)
    part, chunks, dnorm = pl.pallas_call(
        edge_kernel,
        out_shape=(
            jax.ShapeDtypeStruct((shards, chans, atom_count), BF16),
            jax.ShapeDtypeStruct((batches, chunk_rows, chans), F32),
            jax.ShapeDtypeStruct((chans, atom_count), F32),
        ),
        in_specs=[pl.BlockSpec(memory_space=pltpu.SMEM)] + [vmem] * 9,
        out_specs=(vmem,) * 3,
        scratch_shapes=[
            pltpu.VMEM((groups * chans, GROUP), BF16),
            pltpu.VMEM((groups * chans, GROUP), BF16),
            pltpu.VMEM((groups * chans, GROUP), F32),
            pltpu.VMEM((groups * chans, GROUP), F32),
            pltpu.VMEM((chans, chans), F32),
        ],
        compiler_params=pltpu.CompilerParams(vmem_limit_bytes=VMEM_BYTES),
        name="edges",
    )(
        info,
        feats,
        gain_col,
        w_src,
        w_edge,
        w_out,
        src,
        jnp.stack(dst),
        edge_feat.reshape(shards, slots, edge_feat.shape[4]),
        cots,
    )

    given = move(jnp.stack([part[1], part[3]]), "graph", 1)
    far_part = (part[2].astype(F32) + given[1].astype(F32)).astype(BF16)
    arrived = move(far_part, "graph", 2)
    own_part = part[0].astype(F32) + given[0].astype(F32)

    reduced = reduce_chunks(chunks)

    layer_out, grad_atoms = pl.pallas_call(
        atom_kernel,
        out_shape=(
            jax.ShapeDtypeStruct((atom_count, chans), BF16),
            jax.ShapeDtypeStruct((atom_count, chans), BF16),
        ),
        in_specs=[vmem] * 7,
        out_specs=(vmem,) * 2,
        compiler_params=pltpu.CompilerParams(vmem_limit_bytes=VMEM_BYTES),
        name="atoms",
    )(feats, gain_col, w_out, cot, dnorm, own_part, arrived)

    grad_gain = lax.dynamic_slice_in_dim(reduced[3 * rows], batch * rows, rows, 0)
    return (
        layer_out.reshape(atoms.shape),
        grad_atoms.reshape(atoms.shape),
        reduced[:rows],
        reduced[rows : 2 * rows],
        reduced[2 * rows : 3 * rows],
        grad_gain,
    )


def solution(mesh):
    in_specs = (
        P("dp", "graph", None, None),
        P(),
        P(),
        P(),
        P(),
        P("dp", "graph", None, None),
        P("dp", "graph", None, None),
        P("dp", None, None),
        P("dp", "graph", None, None, None),
        P("dp", "graph", None, None),
    )
    out_specs = (
        P("dp", "graph", None, None),
        P("dp", "graph", None, None),
        P("dp", None),
        P("dp", None),
        P("dp", None),
        P("dp"),
    )
    return jax.shard_map(body, mesh=mesh, in_specs=in_specs, out_specs=out_specs, check_vma=False)
```

```python
import functools

import jax
import jax.numpy as jnp
from jax import lax
from jax.experimental import pallas as pl
from jax.experimental.pallas import tpu as pltpu
from jax.sharding import PartitionSpec as P

DEG_NORM = 23
GROUP = 256
BLOCK = 512
F32 = jnp.float32
BF16 = jnp.bfloat16
VMEM_BYTES = 24 * 1024 * 1024
FIRST_VMEM_BYTES = 56 * 1024 * 1024


def dot(a, b):
    return jnp.dot(a, b, preferred_element_type=F32)


def dot_nt(a, b):
    return lax.dot_general(a, b, (((1,), (1,)), ((), ())), preferred_element_type=F32)


def split(x):
    high = x.astype(BF16)
    return high, (x - high.astype(F32)).astype(BF16)


def stack_groups(x, groups):
    return jnp.concatenate([x[:, g * GROUP : (g + 1) * GROUP] for g in range(groups)], axis=0)


def unstack_groups(x, groups):
    rows = x.shape[0] // groups
    return jnp.concatenate([x[g * rows : (g + 1) * rows, :] for g in range(groups)], axis=1)


def spread(x, which, groups):
    return jnp.concatenate([x * (which == g).astype(F32).astype(BF16) for g in range(groups)], axis=0)


def choose(x, which, groups):
    rows = x.shape[0] // groups
    out = x[:rows, :]
    for g in range(1, groups):
        out = jnp.where(which == g, x[g * rows : (g + 1) * rows, :], out)
    return out


def one_hot(low):
    place = lax.broadcasted_iota(jnp.int32, (GROUP, low.shape[1]), 0)
    return jnp.where(place == low, 1.0, 0.0).astype(BF16)


def column(gain):
    return jnp.broadcast_to(gain[...], (gain.shape[1], gain.shape[1])).T[:, :1]


def norm_parts(atoms):
    feats = atoms.astype(F32).T
    inv = lax.rsqrt(jnp.mean(feats * feats, axis=0, keepdims=True) + 1e-06)
    return feats, inv


def peer_of(k):
    me = lax.axis_index("graph")
    return me, me ^ k


def block_of(src, dst, edges, k, block, count):
    me, peer = peer_of(k)
    start = pl.multiple_of(block * BLOCK, BLOCK)
    span = pl.ds(start, BLOCK)
    s = src[pl.ds(peer, 1), span]
    d = dst[pl.ds(me, 1), span]
    live = lax.broadcasted_iota(jnp.int32, (1, BLOCK), 1) + start < count
    s_hot = one_hot(jnp.where(live, s % GROUP, -1))
    d_hot = one_hot(jnp.where(live, d % GROUP, -1))
    return s_hot, s // GROUP, d_hot, d // GROUP, edges[span, :], span


def activate(table, weights, s_hot, s_high, e, groups):
    w_src_t, w_edge_t = weights
    rows = choose(dot(table[...], s_hot), s_high, groups).astype(BF16)
    pre = dot(w_src_t, rows) + dot_nt(w_edge_t, e)
    sig = 0.5 * jnp.tanh(0.5 * pre) + 0.5
    act = pre * sig
    return act, sig + act - act * sig


def blocks_of(count):
    return (count + BLOCK - 1) // BLOCK


class Fetched:
    def __init__(self, source, held, sem):
        self.held = held
        self.copy = pltpu.make_async_copy(source, held, sem)
        self.copy.start()

    def take(self):
        if self.copy is not None:
            self.copy.wait()
            self.copy = None
        return self.held


def with_fetches(kernel, kinds, ks, outs, *refs):
    refs = list(refs)
    ins, refs = refs[: len(kinds)], refs[len(kinds) :]
    results, refs = refs[:outs], refs[outs:]
    given = []
    for ref, kind in zip(ins, kinds):
        if kind == "edges":
            held, sems = refs.pop(0), refs.pop(0)
            given.append([Fetched(ref.at[peer_of(k)[1]], held.at[i], sems.at[i]) for i, k in enumerate(ks)])
        elif kind == "copy":
            given.append(Fetched(ref, refs.pop(0), refs.pop(0)))
        else:
            given.append(ref)
    kernel(ks, *given, *results, *refs)


def back_table(w_out, cot, groups):
    back_t = (dot_nt(w_out[...], cot[...]) * (1.0 / DEG_NORM)).astype(BF16)
    return stack_groups(back_t, groups)


def whole_kernel(
    first, ks, counts, src, dst, edges, cot, w_src, w_edge, w_out, *refs
):
    if first:
        atoms, gain, table, src_sum, edge_sum, out_sum, part, back, agg_sum = refs
    else:
        table, src_in, edge_in, out_in, src_sum, edge_sum, out_sum, part, back, agg_sum = refs
    (k,) = ks
    groups = table.shape[0] // edge_sum.shape[0]
    if first:
        feats, inv = norm_parts(atoms.take()[...])
        table[...] = stack_groups((feats * inv * column(gain.take())).astype(BF16), groups)
        src_sum[...] = jnp.zeros_like(src_sum)
        edge_sum[...] = jnp.zeros_like(edge_sum)
        out_sum[...] = jnp.zeros_like(out_sum)
    else:
        src_sum[...] = src_in[...]
        edge_sum[...] = edge_in[...]
        out_sum[...] = out_in[...]
    cot = cot.take()
    back[...] = back_table(w_out.take(), cot, groups)
    weights = (w_src.take()[...].T, w_edge.take()[...].T)
    agg_sum[...] = jnp.zeros_like(agg_sum)
    src, dst = src.take(), dst.take()
    me, peer = peer_of(k)
    count = counts.take()[me, peer]
    held = edges[0].take()

    def step(block, carry):
        s_hot, s_high, d_hot, d_high, e, _ = block_of(src, dst, held, k, block, count)
        act, slope = activate(table, weights, s_hot, s_high, e, groups)
        agg_sum[...] += dot_nt(spread(act.astype(BF16), d_high, groups), d_hot)
        slot_back = choose(dot(back[...], d_hot), d_high, groups)
        dpre = (slot_back * slope).astype(BF16)
        edge_sum[...] += dot(dpre, e)
        src_sum[...] += dot_nt(spread(dpre, s_high, groups), s_hot)
        return carry

    lax.fori_loop(0, blocks_of(count), step, 0)
    total = unstack_groups(agg_sum[...], groups) * (1.0 / DEG_NORM)
    part_k = total.astype(BF16)
    part[...] = part_k
    out_sum[...] += dot(part_k, cot[...])


def forward_kernel(
    ks, counts, src, dst_a, dst_b, edges, w_src, w_edge, table, part, slopes, agg_sum
):
    groups = table.shape[0] // part.shape[1]
    weights = (w_src.take()[...].T, w_edge.take()[...].T)
    src = src.take()
    counts = counts.take()
    for i, (k, dst) in enumerate(zip(ks, (dst_a, dst_b))):
        me, peer = peer_of(k)
        count = counts[me, peer]
        agg_sum[...] = jnp.zeros_like(agg_sum)
        dst = dst.take()
        held = edges[i].take()

        def step(block, carry, i=i, k=k, dst=dst, count=count, held=held):
            s_hot, s_high, d_hot, d_high, e, span = block_of(src, dst, held, k, block, count)
            act, slope = activate(table, weights, s_hot, s_high, e, groups)
            slopes[i, :, span] = slope
            agg_sum[...] += dot_nt(spread(act.astype(BF16), d_high, groups), d_hot)
            return carry

        lax.fori_loop(0, blocks_of(count), step, 0)
        part[i] = (unstack_groups(agg_sum[...], groups) * (1.0 / DEG_NORM)).astype(BF16)


def backward_kernel(
    ks,
    counts,
    src,
    dst_a,
    dst_b,
    edges,
    cot_a,
    cot_b,
    w_src,
    w_out,
    table,
    slopes,
    part,
    src_in,
    edge_in,
    out_in,
    atoms,
    chunks,
    dnorm_out,
    back,
    src_sum,
    edge_sum,
):
    chans = edge_sum.shape[0]
    groups = table.shape[0] // chans
    w_out = w_out.take()
    src = src.take()
    counts = counts.take()
    src_sum[...] = src_in[...]
    edge_sum[...] = edge_in[...]
    grad_out = out_in[...]
    for i, (k, dst, cot) in enumerate(zip(ks, (dst_a, dst_b), (cot_a, cot_b))):
        me, peer = peer_of(k)
        count = counts[me, peer]
        cot = cot.take()
        back[...] = back_table(w_out, cot, groups)
        dst = dst.take()
        held = edges[i].take()

        def step(block, carry, i=i, k=k, dst=dst, count=count, held=held):
            s_hot, s_high, d_hot, d_high, e, span = block_of(src, dst, held, k, block, count)
            slot_back = choose(dot(back[...], d_hot), d_high, groups)
            dpre = (slot_back * slopes[i, :, span]).astype(BF16)
            edge_sum[...] += dot(dpre, e)
            src_sum[...] += dot_nt(spread(dpre, s_high, groups), s_hot)
            return carry

        lax.fori_loop(0, blocks_of(count), step, 0)
        grad_out = grad_out + dot(part[i], cot[...])
    w_src = w_src.take()
    feats, inv = norm_parts(atoms.take()[...])
    normed = unstack_groups(table[...], groups)
    high, low = split(unstack_groups(src_sum[...], groups))
    grad_src = dot_nt(normed, high) + dot_nt(normed, low)
    dnorm = dot(w_src[...], high) + dot(w_src[...], low)
    dnorm_out[...] = dnorm
    grad_gain = jnp.sum(dnorm * feats * inv, axis=1, keepdims=True)
    grad_gain = jnp.broadcast_to(grad_gain, (chans, chans)).T
    grad_edge = edge_sum[...].T
    batches = chunks.shape[0]
    rows = chans // batches
    mine = lax.axis_index("dp")
    for j in range(batches):
        place = j ^ mine
        for n, grad in enumerate((grad_src, grad_edge, grad_out)):
            chunks[place, n * rows : (n + 1) * rows, :] = grad[j * rows : (j + 1) * rows, :]
        chunks[place, 3 * rows :, :] = grad_gain[: chunks.shape[1] - 3 * rows, :]


def atom_kernel(ks, atoms, gain, w_out, cot, dnorm, agg_a, agg_b, layer_out, grad_atoms):
    feats_rows = atoms.take()[...]
    feats, inv = norm_parts(feats_rows)
    scaled = column(gain.take()) * dnorm[...]
    mean = jnp.mean(feats * scaled, axis=0, keepdims=True)
    rest = inv * scaled - feats * (inv * inv * inv * mean)
    grad_atoms[...] = (cot.take()[...].astype(F32) + rest.T).astype(BF16)
    agg = (agg_a.take()[...].astype(F32) + agg_b.take()[...].astype(F32)).T.astype(BF16)
    layer_out[...] = (feats_rows.astype(F32) + dot(agg, w_out.take()[...])).astype(BF16)


def move(x, axis, bit):
    size = lax.axis_size(axis)
    return lax.ppermute(x, axis, [(i, i ^ bit) for i in range(size)])


def move_both(x, batch_bit, graph_bit):
    batches, shards = lax.axis_size("dp"), lax.axis_size("graph")
    pairs = [
        (b * shards + g, (b ^ batch_bit) * shards + (g ^ graph_bit))
        for b in range(batches)
        for g in range(shards)
    ]
    return lax.ppermute(x, ("dp", "graph"), pairs)


def reduce_chunks(chunks):
    batches, rows, width = chunks.shape
    total = chunks + move(chunks, "graph", 1)
    pair = total.reshape(batches // 2, 2, rows, width)
    keep, give = pair[:, 0], pair[:, 1]
    total = keep + move(keep, "graph", 2) + move(give, "dp", 1) + move_both(give, 1, 2)
    bit = 2
    while bit < batches:
        left = batches // bit
        fan = min(4, left)
        parts = total.reshape(left // fan, fan, rows, width)
        total = parts[:, 0]
        for k in range(1, fan):
            total = total + move(parts[:, k], "dp", k * bit)
        bit *= fan
    return total.reshape(rows, width)


def body(atoms, gain, w_src, w_edge, w_out, send_src, recv_dst, edge_count, edge_feat, cotangent):
    shards = lax.axis_size("graph")
    batches = lax.axis_size("dp")
    batch = lax.axis_index("dp")
    atom_count, chans = atoms.shape[2:]
    slots = send_src.shape[3]
    groups = atom_count // GROUP
    feats = atoms.reshape(atom_count, chans)
    src = send_src.reshape(shards, slots)
    dst_here = recv_dst.reshape(shards, slots)
    cot = cotangent.reshape(atom_count, chans)
    gain_row = gain.reshape(1, chans)
    edges = edge_feat.reshape(shards, slots, edge_feat.shape[4])
    counts = edge_count.reshape(shards, shards)

    dst = [dst_here] + [move(dst_here, "graph", k) for k in range(1, shards)]
    far = move(cot, "graph", 2)
    cots = [cot, move(cot, "graph", 1), far, move(far, "graph", 1)]

    vmem = pl.BlockSpec(memory_space=pltpu.VMEM)
    hbm = pl.BlockSpec(memory_space=pl.ANY)

    def call(kernel, ks, outs, ins, scratch, name, flops):
        kinds = ["edges" if x is edges else "copy" if id(x) in copied else "here" for x in ins]
        buffers = []
        for x, kind in zip(ins, kinds):
            if kind == "edges":
                buffers += [pltpu.VMEM((len(ks),) + x.shape[1:], x.dtype), pltpu.SemaphoreType.DMA((len(ks),))]
            elif kind == "copy":
                space = pltpu.SMEM if x is counts else pltpu.VMEM
                buffers += [space(x.shape, x.dtype), pltpu.SemaphoreType.DMA]
        return pl.pallas_call(
            functools.partial(with_fetches, kernel, kinds, ks, len(outs)),
            out_shape=tuple(jax.ShapeDtypeStruct(shape, kind) for shape, kind in outs),
            in_specs=[vmem if kind == "here" else hbm for kind in kinds],
            out_specs=(vmem,) * len(outs),
            scratch_shapes=buffers + scratch,
            compiler_params=pltpu.CompilerParams(
                vmem_limit_bytes=FIRST_VMEM_BYTES if name == "own_edges" else VMEM_BYTES
            ),
            cost_estimate=pl.CostEstimate(flops=flops, bytes_accessed=1 << 20, transcendentals=0),
            name=name,
        )(*ins)

    copied = {id(x) for x in [counts, src, w_src, w_edge, w_out, feats, gain_row] + dst + cots}
    tall = (groups * chans, GROUP)
    square = (chans, chans)
    sums = [(tall, F32), (square, F32), (square, F32)]
    part_shape = (chans, atom_count)
    table_bf = pltpu.VMEM(tall, BF16)
    table_f32 = pltpu.VMEM(tall, F32)
    unit = 2 * slots * atom_count * chans
    table, src_sum, edge_sum, out_sum, part_0 = call(
        functools.partial(whole_kernel, True),
        (0,),
        [(tall, BF16)] + sums + [(part_shape, BF16)],
        [counts, src, dst[0], edges, cots[0], w_src, w_edge, w_out, feats, gain_row],
        [table_bf, table_f32],
        "own_edges",
        4 * unit,
    )
    far_ks = (2, 3)
    far_parts, slopes = call(
        forward_kernel,
        far_ks,
        [((2,) + part_shape, BF16), ((2, chans, slots), F32)],
        [counts, src, dst[2], dst[3], edges, w_src, w_edge, table],
        [table_f32],
        "far_forward",
        4 * unit,
    )
    src_sum, edge_sum, out_sum, part_1 = call(
        functools.partial(whole_kernel, False),
        (1,),
        sums + [(part_shape, BF16)],
        [counts, src, dst[1], edges, cots[1], w_src, w_edge, w_out, table, src_sum, edge_sum, out_sum],
        [table_bf, table_f32],
        "near_edges",
        4 * unit,
    )
    rows = chans // batches
    chunk_rows = -(-(3 * rows + 1) // 8) * 8
    chunks, dnorm = call(
        backward_kernel,
        far_ks,
        [((batches, chunk_rows, chans), F32), ((chans, atom_count), F32)],
        [counts, src, dst[2], dst[3], edges, cots[2], cots[3], w_src, w_out, table, slopes, far_parts]
        + [src_sum, edge_sum, out_sum, feats],
        [table_bf, table_f32, pltpu.VMEM(square, F32)],
        "far_backward",
        4 * unit,
    )

    given_far = move(far_parts[1], "graph", 1)
    far_part = (far_parts[0].astype(F32) + given_far.astype(F32)).astype(BF16)
    arrived = move(far_part, "graph", 2)
    own_part = part_0.astype(F32) + move(part_1, "graph", 1).astype(F32)

    reduced = reduce_chunks(chunks)

    copied |= {id(own_part), id(arrived)}
    layer_out, grad_atoms = call(
        atom_kernel,
        (),
        [(feats.shape, BF16)] * 2,
        [feats, gain_row, w_out, cot, dnorm, own_part, arrived],
        [],
        "atoms",
        unit // 8,
    )

    grad_gain = lax.dynamic_slice_in_dim(reduced[3 * rows], batch * rows, rows, 0)
    return (
        layer_out.reshape(atoms.shape),
        grad_atoms.reshape(atoms.shape),
        reduced[:rows],
        reduced[rows : 2 * rows],
        reduced[2 * rows : 3 * rows],
        grad_gain,
    )


def solution(mesh):
    in_specs = (
        P("dp", "graph", None, None),
        P(),
        P(),
        P(),
        P(),
        P("dp", "graph", None, None),
        P("dp", "graph", None, None),
        P("dp", None, None),
        P("dp", "graph", None, None, None),
        P("dp", "graph", None, None),
    )
    out_specs = (
        P("dp", "graph", None, None),
        P("dp", "graph", None, None),
        P("dp", None),
        P("dp", None),
        P("dp", None),
        P("dp"),
    )
    return jax.shard_map(body, mesh=mesh, in_specs=in_specs, out_specs=out_specs, check_vma=False)
```

```python
import functools

import jax
import jax.numpy as jnp
from jax import lax
from jax.experimental import pallas as pl
from jax.experimental.pallas import tpu as pltpu
from jax.sharding import PartitionSpec as P

DEG_NORM = 23
GROUP = 256
BLOCK = 1024
F32 = jnp.float32
BF16 = jnp.bfloat16
FAR_VMEM_BYTES = 24 * 1024 * 1024
NEAR_VMEM_BYTES = 56 * 1024 * 1024


def dot(a, b):
    return jnp.dot(a, b, preferred_element_type=F32)


def dot_nt(a, b):
    return lax.dot_general(a, b, (((1,), (1,)), ((), ())), preferred_element_type=F32)


def split(x):
    high = x.astype(BF16)
    return high, (x - high.astype(F32)).astype(BF16)


def stack_groups(x, groups):
    return jnp.concatenate([x[:, g * GROUP : (g + 1) * GROUP] for g in range(groups)], axis=0)


def unstack_groups(x, groups):
    rows = x.shape[0] // groups
    return jnp.concatenate([x[g * rows : (g + 1) * rows, :] for g in range(groups)], axis=1)


def spread(x, which, groups):
    return jnp.concatenate([x * (which == g).astype(F32).astype(BF16) for g in range(groups)], axis=0)


def choose(x, which, groups):
    rows = x.shape[0] // groups
    out = x[:rows, :]
    for g in range(1, groups):
        out = jnp.where(which == g, x[g * rows : (g + 1) * rows, :], out)
    return out


def one_hot(low):
    place = lax.broadcasted_iota(jnp.int32, (GROUP, low.shape[1]), 0)
    return jnp.where(place == low, 1.0, 0.0).astype(BF16)


def column(gain):
    return jnp.broadcast_to(gain[...], (gain.shape[1], gain.shape[1])).T[:, :1]


def norm_parts(atoms):
    feats = atoms.astype(F32).T
    inv = lax.rsqrt(jnp.mean(feats * feats, axis=0, keepdims=True) + 1e-06)
    return feats, inv


def peer_of(k):
    return lax.axis_index("graph") ^ k


class Fetched:
    def __init__(self, source, held, sem):
        self.held = held
        self.copy = pltpu.make_async_copy(source, held, sem)
        self.copy.start()

    def take(self):
        if self.copy is not None:
            self.copy.wait()
            self.copy = None
        return self.held


class Many:
    def __init__(self, moves, held):
        self.held = held
        self.parts = [Fetched(*move) for move in moves]

    def take(self):
        for part in self.parts:
            part.take()
        return self.held


def with_fetches(kernel, kinds, ks, outs, *refs):
    refs = list(refs)
    count = sum(len(ks) if kind == "many" else 1 for kind in kinds)
    ins, refs = refs[:count], refs[count:]
    results, refs = refs[:outs], refs[outs:]
    given = []
    ins = iter(ins)
    for kind in kinds:
        ref = next(ins)
        if kind == "many":
            held, sems = refs.pop(0), refs.pop(0)
            sources = [ref] + [next(ins) for _ in ks[1:]]
            given.append(Many([(x, held.at[i], sems.at[i]) for i, x in enumerate(sources)], held))
        elif kind == "edges":
            held, sems = refs.pop(0), refs.pop(0)
            given.append(Many([(ref.at[peer_of(k)], held.at[i], sems.at[i]) for i, k in enumerate(ks)], held))
        elif kind == "copy":
            given.append(Fetched(ref, refs.pop(0), refs.pop(0)))
        else:
            given.append(ref)
    kernel(ks, *given, *results, *refs)


def back_table(w_out, cot, groups):
    back_t = (dot_nt(w_out[...], cot[...]) * (1.0 / DEG_NORM)).astype(BF16)
    return stack_groups(back_t, groups)


def run_blocks(ks, counts, src, dsts, edges, table, back, w_src_t, w_edge_t, agg_sum, src_sum, edge_sum, hold):
    groups = back.shape[1] // edge_sum.shape[0]
    me = lax.axis_index("graph")
    sizes = [counts[me, peer_of(k)] for k in ks]
    firsts = [0]
    for size in sizes:
        firsts.append(firsts[-1] + (size + BLOCK - 1) // BLOCK)
    total = firsts[-1]

    def locate(item):
        i = jnp.int32(0)
        first = jnp.int32(0)
        peer = peer_of(ks[0])
        size = sizes[0]
        for j in range(1, len(ks)):
            past = item >= firsts[j]
            i = jnp.where(past, j, i)
            first = jnp.where(past, firsts[j], first)
            peer = jnp.where(past, peer_of(ks[j]), peer)
            size = jnp.where(past, sizes[j], size)
        start = pl.multiple_of((item - first) * BLOCK, BLOCK)
        span = pl.ds(start, BLOCK)
        live = lax.broadcasted_iota(jnp.int32, (1, BLOCK), 1) + start < size
        s = src[pl.ds(peer, 1), span]
        d = dsts[i, pl.ds(me, 1), span]
        s_low = jnp.where(live, s % GROUP, -1)
        d_low = jnp.where(live, d % GROUP, -1)
        return i, span, s_low, s // GROUP, d_low, d // GROUP

    def gather(item):
        i, span, s_low, s_high, d_low, d_high = locate(item)
        rows = choose(dot(table[...], one_hot(s_low)), s_high, groups).astype(BF16)
        pre = dot(w_src_t, rows) + dot_nt(w_edge_t, edges[i, span, :])
        slot_back = choose(dot(back[i], one_hot(d_low)), d_high, groups)
        sig = 0.5 * jnp.tanh(0.5 * pre) + 0.5
        act = pre * sig
        slope = sig + act - act * sig
        return act.astype(BF16), (slot_back * slope).astype(BF16)

    def scatter(item, msg, dpre):
        i, span, s_low, s_high, d_low, d_high = locate(item)
        agg_sum[i] += dot_nt(spread(msg, d_high, groups), one_hot(d_low))
        edge_sum[...] += dot(dpre, edges[i, span, :])
        src_sum[...] += dot_nt(spread(dpre, s_high, groups), one_hot(s_low))

    def step(item, carry):
        msg, dpre = hold[0], hold[1]
        next_msg, next_dpre = gather(item)
        scatter(item - 1, msg, dpre)
        hold[0] = next_msg
        hold[1] = next_dpre
        return carry

    @pl.when(total > 0)
    def _():
        msg, dpre = gather(0)
        hold[0] = msg
        hold[1] = dpre

    lax.fori_loop(1, total, step, 0)

    @pl.when(total > 0)
    def _():
        scatter(total - 1, hold[0], hold[1])


def slots_of(ks, refs, table, back, parts, agg_sum, src_sum, edge_sum, out_sum, hold):
    w_out, cots, w_src, w_edge, counts, src, dsts, edges = refs
    groups = back.shape[1] // edge_sum.shape[0]
    w_out = w_out.take()
    cots = cots.take()
    for i in range(len(ks)):
        back[i] = back_table(w_out, cots.at[i], groups)
    agg_sum[...] = jnp.zeros_like(agg_sum)
    w_src_t, w_edge_t = w_src.take()[...].T, w_edge.take()[...].T
    counts, src = counts.take(), src.take()
    dsts, edges = dsts.take(), edges.take()
    run_blocks(
        ks, counts, src, dsts, edges, table, back, w_src_t, w_edge_t, agg_sum, src_sum, edge_sum, hold
    )
    for i in range(len(ks)):
        part = (unstack_groups(agg_sum[i], groups) * (1.0 / DEG_NORM)).astype(BF16)
        parts[i] = part
        out_sum[...] += dot(part, cots[i])


def three_sums(sums, chans):
    tall = sums.shape[0] - chans
    return sums.at[:tall], sums.at[tall:, :chans], sums.at[tall:, chans:]


def near_kernel(ks, *refs):
    atoms, gain, *fetched = refs[:10]
    sums, parts, table, back, agg_sum, hold = refs[10:]
    sums[...] = jnp.zeros_like(sums)
    feats, inv = norm_parts(atoms.take()[...])
    table[...] = stack_groups((feats * inv * column(gain.take())).astype(BF16), back.shape[1] // parts.shape[1])
    slots_of(ks, fetched, table, back, parts, agg_sum, *three_sums(sums, parts.shape[1]), hold)


def far_kernel(ks, *refs):
    atoms, gain, *fetched = refs[:10]
    sums, parts, chunks, dnorm_out, table, back, agg_sum, hold = refs[10:]
    chans = parts.shape[1]
    groups = back.shape[1] // chans
    feats, inv = norm_parts(atoms.take()[...])
    normed = (feats * inv * column(gain.take())).astype(BF16)
    table[...] = stack_groups(normed, groups)
    src_sum, edge_sum, out_sum = three_sums(sums.take(), chans)
    slots_of(ks, fetched, table, back, parts, agg_sum, src_sum, edge_sum, out_sum, hold)
    w_src = fetched[2].take()
    high, low = split(unstack_groups(src_sum[...], groups))
    grad_src = dot_nt(normed, high) + dot_nt(normed, low)
    dnorm = dot(w_src[...], high) + dot(w_src[...], low)
    dnorm_out[...] = dnorm
    grad_gain = jnp.sum(dnorm * feats * inv, axis=1, keepdims=True)
    grad_gain = jnp.broadcast_to(grad_gain, (chans, chans)).T
    grad_edge = edge_sum[...].T
    grad_out = out_sum[...]
    batches = chunks.shape[0]
    rows = chans // batches
    mine = lax.axis_index("dp")
    for j in range(batches):
        place = j ^ mine
        for n, grad in enumerate((grad_src, grad_edge, grad_out)):
            chunks[place, n * rows : (n + 1) * rows, :] = grad[j * rows : (j + 1) * rows, :]
        chunks[place, 3 * rows :, :] = grad_gain[: chunks.shape[1] - 3 * rows, :]


def atom_kernel(ks, atoms, gain, w_out, cot, dnorm, agg_a, agg_b, layer_out, grad_atoms):
    feats_rows = atoms.take()[...]
    feats, inv = norm_parts(feats_rows)
    scaled = column(gain.take()) * dnorm.take()[...]
    mean = jnp.mean(feats * scaled, axis=0, keepdims=True)
    rest = inv * scaled - feats * (inv * inv * inv * mean)
    grad_atoms[...] = (cot.take()[...].astype(F32) + rest.T).astype(BF16)
    agg = (agg_a.take()[...].astype(F32) + agg_b.take()[...].astype(F32)).T.astype(BF16)
    layer_out[...] = (feats_rows.astype(F32) + dot(agg, w_out.take()[...])).astype(BF16)


def move(x, axis, bit):
    size = lax.axis_size(axis)
    return lax.ppermute(x, axis, [(i, i ^ bit) for i in range(size)])


def reduce_batches(chunks, bits):
    for _ in range(bits):
        batches, rows, width = chunks.shape
        bit = lax.axis_size("dp") // batches
        pair = chunks.reshape(batches // 2, 2, rows, width)
        chunks = pair[:, 0] + move(pair[:, 1], "dp", bit)
    return chunks


def body(atoms, gain, w_src, w_edge, w_out, send_src, recv_dst, edge_count, edge_feat, cotangent):
    shards = lax.axis_size("graph")
    batches = lax.axis_size("dp")
    batch = lax.axis_index("dp")
    atom_count, chans = atoms.shape[2:]
    slots = send_src.shape[3]
    groups = atom_count // GROUP
    feats = atoms.reshape(atom_count, chans)
    src = send_src.reshape(shards, slots)
    dst_here = recv_dst.reshape(shards, slots)
    cot = cotangent.reshape(atom_count, chans)
    gain_row = gain.reshape(1, chans)
    edges = edge_feat.reshape(shards, slots, edge_feat.shape[4])
    counts = edge_count.reshape(shards, shards)

    far_dst = move(dst_here, "graph", 2)
    far = move(cot, "graph", 2)
    dst = [dst_here, move(dst_here, "graph", 1)]
    src, far_dst = lax.optimization_barrier((src, far_dst))
    cots = [cot, move(cot, "graph", 1), far]

    vmem = pl.BlockSpec(memory_space=pltpu.VMEM)
    hbm = pl.BlockSpec(memory_space=pltpu.HBM)

    def call(kernel, ks, outs, ins, scratch, name, flops, limit):
        kinds, flat, buffers = [], [], []
        for x in ins:
            if isinstance(x, list):
                kinds.append("many")
                flat += x
                buffers += [pltpu.VMEM((len(x),) + x[0].shape, x[0].dtype), pltpu.SemaphoreType.DMA((len(x),))]
            elif x is edges:
                kinds.append("edges")
                flat.append(x)
                buffers += [pltpu.VMEM((len(ks),) + x.shape[1:], x.dtype), pltpu.SemaphoreType.DMA((len(ks),))]
            elif id(x) in here:
                kinds.append("here")
                flat.append(x)
            else:
                kinds.append("copy")
                flat.append(x)
                space = pltpu.SMEM if x is counts else pltpu.VMEM
                buffers += [space(x.shape, x.dtype), pltpu.SemaphoreType.DMA]
        return pl.pallas_call(
            functools.partial(with_fetches, kernel, kinds, ks, len(outs)),
            out_shape=tuple(jax.ShapeDtypeStruct(shape, kind) for shape, kind in outs),
            in_specs=[vmem if id(x) in here else hbm for x in flat],
            out_specs=(vmem,) * len(outs),
            scratch_shapes=buffers + scratch,
            compiler_params=pltpu.CompilerParams(vmem_limit_bytes=limit),
            cost_estimate=pl.CostEstimate(flops=flops, bytes_accessed=1 << 20, transcendentals=0),
            name=name,
        )(*flat)

    here = set()
    tall = (groups * chans, GROUP)
    sums_shape = (groups * chans + chans, GROUP)
    part_shape = (chans, atom_count)
    unit = 2 * slots * atom_count * chans

    def work(ks):
        return [
            pltpu.VMEM(tall, BF16),
            pltpu.VMEM((len(ks),) + tall, BF16),
            pltpu.VMEM((len(ks),) + tall, F32),
            pltpu.VMEM((2, chans, BLOCK), BF16),
        ]

    near, distant = (0, 1), (2, 3)
    sums, near_parts = call(
        near_kernel,
        near,
        [(sums_shape, F32), ((2,) + part_shape, BF16)],
        [feats, gain_row, w_out, cots[:2], w_src, w_edge, counts, src, dst[:2], edges],
        work(near),
        "near_edges",
        8 * unit,
        NEAR_VMEM_BYTES,
    )
    far, far_dst, sums = lax.optimization_barrier((far, far_dst, sums))
    dst = dst + [far_dst, move(far_dst, "graph", 1)]
    cots = cots[:2] + [far, move(far, "graph", 1)]
    rows = chans // batches
    chunk_rows = -(-(3 * rows + 1) // 8) * 8
    far_parts, chunks, dnorm = call(
        far_kernel,
        distant,
        [((2,) + part_shape, BF16), ((batches, chunk_rows, chans), F32), ((chans, atom_count), F32)],
        [feats, gain_row, w_out, cots[2:], w_src, w_edge, counts, src, dst[2:], edges, sums],
        work(distant),
        "far_edges",
        8 * unit,
        FAR_VMEM_BYTES,
    )

    given_far = move(far_parts[1], "graph", 1)
    chunks = reduce_batches(chunks, 1)
    chunks, given_far = lax.optimization_barrier((chunks, given_far))
    far_part = (far_parts[0].astype(F32) + given_far.astype(F32)).astype(BF16)
    arrived = move(far_part, "graph", 2)
    own_part = near_parts[0].astype(F32) + move(near_parts[1], "graph", 1).astype(F32)
    chunks = reduce_batches(chunks, batches.bit_length() - 2)
    chunks, arrived = lax.optimization_barrier((chunks, arrived))
    total = chunks.reshape(chunk_rows, chans)
    total = total + move(total, "graph", 2)

    layer_out, grad_atoms = call(
        atom_kernel,
        (),
        [(feats.shape, BF16)] * 2,
        [feats, gain_row, w_out, cot, dnorm, own_part, arrived],
        [],
        "atoms",
        unit // 8,
        FAR_VMEM_BYTES,
    )

    total, layer_out, grad_atoms = lax.optimization_barrier((total, layer_out, grad_atoms))
    reduced = total + move(total, "graph", 1)
    grad_gain = lax.dynamic_slice_in_dim(reduced[3 * rows], batch * rows, rows, 0)
    return (
        layer_out.reshape(atoms.shape),
        grad_atoms.reshape(atoms.shape),
        reduced[:rows],
        reduced[rows : 2 * rows],
        reduced[2 * rows : 3 * rows],
        grad_gain,
    )


def solution(mesh):
    in_specs = (
        P("dp", "graph", None, None),
        P(),
        P(),
        P(),
        P(),
        P("dp", "graph", None, None),
        P("dp", "graph", None, None),
        P("dp", None, None),
        P("dp", "graph", None, None, None),
        P("dp", "graph", None, None),
    )
    out_specs = (
        P("dp", "graph", None, None),
        P("dp", "graph", None, None),
        P("dp", None),
        P("dp", None),
        P("dp", None),
        P("dp"),
    )
    return jax.shard_map(body, mesh=mesh, in_specs=in_specs, out_specs=out_specs, check_vma=False)
```

```python
import functools

import jax
import jax.numpy as jnp
from jax import lax
from jax.experimental import pallas as pl
from jax.experimental.pallas import tpu as pltpu
from jax.sharding import PartitionSpec as P

DEG_NORM = 23
GROUP = 256
BLOCK = 1024
F32 = jnp.float32
BF16 = jnp.bfloat16
FAR_VMEM_BYTES = 24 * 1024 * 1024
NEAR_VMEM_BYTES = 56 * 1024 * 1024


def dot(a, b):
    return jnp.dot(a, b, preferred_element_type=F32)


def dot_nt(a, b):
    return lax.dot_general(a, b, (((1,), (1,)), ((), ())), preferred_element_type=F32)


def split(x):
    high = x.astype(BF16)
    return high, (x - high.astype(F32)).astype(BF16)


def stack_groups(x, groups):
    return jnp.concatenate([x[:, g * GROUP : (g + 1) * GROUP] for g in range(groups)], axis=0)


def unstack_groups(x, groups):
    rows = x.shape[0] // groups
    return jnp.concatenate([x[g * rows : (g + 1) * rows, :] for g in range(groups)], axis=1)


def spread(x, which, groups):
    return jnp.concatenate([x * (which == g).astype(F32).astype(BF16) for g in range(groups)], axis=0)


def choose(x, which, groups):
    rows = x.shape[0] // groups
    out = x[:rows, :]
    for g in range(1, groups):
        out = jnp.where(which == g, x[g * rows : (g + 1) * rows, :], out)
    return out


def one_hot(low):
    place = lax.broadcasted_iota(jnp.int32, (GROUP, low.shape[1]), 0)
    return jnp.where(place == low, 1.0, 0.0).astype(BF16)


def column(gain):
    return jnp.broadcast_to(gain[...], (gain.shape[1], gain.shape[1])).T[:, :1]


def norm_parts(atoms):
    feats = atoms.astype(F32).T
    inv = lax.rsqrt(jnp.mean(feats * feats, axis=0, keepdims=True) + 1e-06)
    return feats, inv


def peer_of(k):
    return lax.axis_index("graph") ^ k


class Fetched:
    def __init__(self, source, held, sem):
        self.held = held
        self.copy = pltpu.make_async_copy(source, held, sem)
        self.copy.start()

    def take(self):
        if self.copy is not None:
            self.copy.wait()
            self.copy = None
        return self.held


class Many:
    def __init__(self, moves, held):
        self.held = held
        self.parts = [Fetched(*move) for move in moves]

    def take(self):
        for part in self.parts:
            part.take()
        return self.held


def with_fetches(kernel, kinds, ks, outs, *refs):
    refs = list(refs)
    count = sum(len(ks) if kind == "many" else 1 for kind in kinds)
    ins, refs = refs[:count], refs[count:]
    results, refs = refs[:outs], refs[outs:]
    given = []
    ins = iter(ins)
    for kind in kinds:
        ref = next(ins)
        if kind == "many":
            held, sems = refs.pop(0), refs.pop(0)
            sources = [ref] + [next(ins) for _ in ks[1:]]
            given.append(Many([(x, held.at[i], sems.at[i]) for i, x in enumerate(sources)], held))
        elif kind == "edges":
            held, sems = refs.pop(0), refs.pop(0)
            given.append(Many([(ref.at[peer_of(k)], held.at[i], sems.at[i]) for i, k in enumerate(ks)], held))
        elif kind == "copy":
            given.append(Fetched(ref, refs.pop(0), refs.pop(0)))
        else:
            given.append(ref)
    kernel(ks, *given, *results, *refs)


def back_table(w_out, cot, groups):
    back_t = (dot_nt(w_out[...], cot[...]) * (1.0 / DEG_NORM)).astype(BF16)
    return stack_groups(back_t, groups)


def run_blocks(ks, counts, src, dsts, edges, table, back, w_src_t, w_edge_t, agg_sum, src_sum, edge_sum, hold):
    groups = back.shape[1] // edge_sum.shape[0]
    me = lax.axis_index("graph")
    sizes = [counts[me, peer_of(k)] for k in ks]
    firsts = [0]
    for size in sizes:
        firsts.append(firsts[-1] + (size + BLOCK - 1) // BLOCK)
    total = firsts[-1]

    def locate(item):
        i = jnp.int32(0)
        first = jnp.int32(0)
        peer = peer_of(ks[0])
        size = sizes[0]
        for j in range(1, len(ks)):
            past = item >= firsts[j]
            i = jnp.where(past, j, i)
            first = jnp.where(past, firsts[j], first)
            peer = jnp.where(past, peer_of(ks[j]), peer)
            size = jnp.where(past, sizes[j], size)
        start = pl.multiple_of((item - first) * BLOCK, BLOCK)
        span = pl.ds(start, BLOCK)
        live = lax.broadcasted_iota(jnp.int32, (1, BLOCK), 1) + start < size
        s = src[pl.ds(peer, 1), span]
        d = dsts[i, pl.ds(me, 1), span]
        s_low = jnp.where(live, s % GROUP, -1)
        d_low = jnp.where(live, d % GROUP, -1)
        return i, span, s_low, s // GROUP, d_low, d // GROUP

    def gather(item):
        i, span, s_low, s_high, d_low, d_high = locate(item)
        rows = choose(dot(table[...], one_hot(s_low)), s_high, groups).astype(BF16)
        pre = dot(w_src_t, rows) + dot_nt(w_edge_t, edges[i, span, :])
        slot_back = choose(dot(back[i], one_hot(d_low)), d_high, groups)
        sig = 0.5 * jnp.tanh(0.5 * pre) + 0.5
        act = pre * sig
        slope = sig + act - act * sig
        return act.astype(BF16), (slot_back * slope).astype(BF16)

    def scatter(item, msg, dpre):
        i, span, s_low, s_high, d_low, d_high = locate(item)
        agg_sum[i] += dot_nt(spread(msg, d_high, groups), one_hot(d_low))
        edge_sum[...] += dot(dpre, edges[i, span, :])
        src_sum[...] += dot_nt(spread(dpre, s_high, groups), one_hot(s_low))

    def step(item, carry):
        msg, dpre = hold[0], hold[1]
        next_msg, next_dpre = gather(item)
        scatter(item - 1, msg, dpre)
        hold[0] = next_msg
        hold[1] = next_dpre
        return carry

    @pl.when(total > 0)
    def _():
        msg, dpre = gather(0)
        hold[0] = msg
        hold[1] = dpre

    lax.fori_loop(1, total, step, 0)

    @pl.when(total > 0)
    def _():
        scatter(total - 1, hold[0], hold[1])


def slots_of(ks, refs, table, back, parts, agg_sum, src_sum, edge_sum, out_sum, hold):
    w_out, cots, w_src, w_edge, counts, src, dsts, edges = refs
    groups = back.shape[1] // edge_sum.shape[0]
    w_out = w_out.take()
    cots = cots.take()
    for i in range(len(ks)):
        back[i] = back_table(w_out, cots.at[i], groups)
    agg_sum[...] = jnp.zeros_like(agg_sum)
    w_src_t, w_edge_t = w_src.take()[...].T, w_edge.take()[...].T
    counts, src = counts.take(), src.take()
    dsts, edges = dsts.take(), edges.take()
    run_blocks(
        ks, counts, src, dsts, edges, table, back, w_src_t, w_edge_t, agg_sum, src_sum, edge_sum, hold
    )
    for i in range(len(ks)):
        part = (unstack_groups(agg_sum[i], groups) * (1.0 / DEG_NORM)).astype(BF16)
        parts[i] = part
        out_sum[...] += dot(part, cots[i])


def edge_kernel(ks, *refs):
    atoms, gain, *fetched = refs[:10]
    parts, chunks, src_sum, table, back, agg_sum, edge_sum, out_sum, hold = refs[10:]
    chans = edge_sum.shape[0]
    groups = back.shape[1] // chans
    src_sum[...] = jnp.zeros_like(src_sum)
    edge_sum[...] = jnp.zeros_like(edge_sum)
    out_sum[...] = jnp.zeros_like(out_sum)
    feats, inv = norm_parts(atoms.take()[...])
    normed = (feats * inv * column(gain.take())).astype(BF16)
    table[...] = stack_groups(normed, groups)
    slots_of(ks, fetched, table, back, parts, agg_sum, src_sum, edge_sum, out_sum, hold)
    high, low = split(unstack_groups(src_sum[...], groups))
    normed = unstack_groups(table[...], groups)
    grad_src = dot_nt(normed, high) + dot_nt(normed, low)
    grad_edge = edge_sum[...].T
    grad_out = out_sum[...]
    batches = chunks.shape[0]
    rows = chans // batches
    left = chunks.shape[1] - 3 * rows
    mine = lax.axis_index("dp")
    for j in range(batches):
        place = j ^ mine
        for n, grad in enumerate((grad_src, grad_edge, grad_out)):
            chunks[place, n * rows : (n + 1) * rows, :] = grad[j * rows : (j + 1) * rows, :]
        if left:
            chunks[place, 3 * rows :, :] = jnp.zeros((left, chans), F32)


def atom_kernel(ks, atoms, gain, w_src, w_out, cot, sum_a, sum_b, agg_a, agg_b, layer_out, grad_atoms):
    feats_rows = atoms.take()[...]
    feats, inv = norm_parts(feats_rows)
    groups = feats_rows.shape[0] // GROUP
    high, low = split(unstack_groups(sum_a.take()[...] + sum_b.take()[...], groups))
    w_src = w_src.take()[...]
    scaled = column(gain.take()) * (dot(w_src, high) + dot(w_src, low))
    mean = jnp.mean(feats * scaled, axis=0, keepdims=True)
    rest = inv * scaled - feats * (inv * inv * inv * mean)
    grad_atoms[...] = (cot.take()[...].astype(F32) + rest.T).astype(BF16)
    agg = (agg_a.take()[...].astype(F32) + agg_b.take()[...].astype(F32)).T.astype(BF16)
    layer_out[...] = (feats_rows.astype(F32) + dot(agg, w_out.take()[...])).astype(BF16)


def weight_kernel(ks, ours, theirs, w_src, gain, grad_src, grad_edge, grad_out, grad_gain):
    rows, chans = grad_src.shape
    total = ours[...] + theirs[...]
    for n, out in enumerate((grad_src, grad_edge, grad_out)):
        out[...] = total[n * rows : (n + 1) * rows, :]
    place = lax.broadcasted_iota(jnp.int32, (rows, chans), 1)
    row = lax.broadcasted_iota(jnp.int32, (rows, chans), 0)
    mine = place == row + lax.axis_index("dp") * rows
    w_rows = dot(jnp.where(mine, 1.0, 0.0).astype(BF16), w_src.take()[...])
    gains = jnp.sum(jnp.where(mine, gain.take()[...], 0.0), axis=1, keepdims=True)
    value = jnp.sum(w_rows * total[:rows, :], axis=1, keepdims=True) / gains
    grad_gain[...] = jnp.sum(jnp.where(place == row, value, 0.0), axis=0, keepdims=True)[:, :rows]


def move(x, axis, bit):
    size = lax.axis_size(axis)
    return lax.ppermute(x, axis, [(i, i ^ bit) for i in range(size)])


def reduce_batches(chunks, bits):
    for _ in range(bits):
        batches, rows, width = chunks.shape
        bit = lax.axis_size("dp") // batches
        pair = chunks.reshape(batches // 2, 2, rows, width)
        chunks = pair[:, 0] + move(pair[:, 1], "dp", bit)
    return chunks


def body(atoms, gain, w_src, w_edge, w_out, send_src, recv_dst, edge_count, edge_feat, cotangent):
    shards = lax.axis_size("graph")
    batches = lax.axis_size("dp")
    atom_count, chans = atoms.shape[2:]
    slots = send_src.shape[3]
    groups = atom_count // GROUP
    feats = atoms.reshape(atom_count, chans)
    src = send_src.reshape(shards, slots)
    dst_here = recv_dst.reshape(shards, slots)
    cot = cotangent.reshape(atom_count, chans)
    gain_row = gain.reshape(1, chans)
    edges = edge_feat.reshape(shards, slots, edge_feat.shape[4])
    counts = edge_count.reshape(shards, shards)

    far_dst = move(dst_here, "graph", 2)
    far = move(cot, "graph", 2)
    dst = [dst_here, move(dst_here, "graph", 1)]
    cots = [cot, move(cot, "graph", 1), far]

    vmem = pl.BlockSpec(memory_space=pltpu.VMEM)
    hbm = pl.BlockSpec(memory_space=pltpu.HBM)

    def call(kernel, ks, outs, ins, scratch, name, flops, limit):
        kinds, flat, buffers = [], [], []
        for x in ins:
            if isinstance(x, list):
                kinds.append("many")
                flat += x
                buffers += [pltpu.VMEM((len(x),) + x[0].shape, x[0].dtype), pltpu.SemaphoreType.DMA((len(x),))]
            elif x is edges:
                kinds.append("edges")
                flat.append(x)
                buffers += [pltpu.VMEM((len(ks),) + x.shape[1:], x.dtype), pltpu.SemaphoreType.DMA((len(ks),))]
            elif id(x) in here:
                kinds.append("here")
                flat.append(x)
            else:
                kinds.append("copy")
                flat.append(x)
                space = pltpu.SMEM if x is counts else pltpu.VMEM
                buffers += [space(x.shape, x.dtype), pltpu.SemaphoreType.DMA]
        return pl.pallas_call(
            functools.partial(with_fetches, kernel, kinds, ks, len(outs)),
            out_shape=tuple(jax.ShapeDtypeStruct(shape, kind) for shape, kind in outs),
            in_specs=[vmem if id(x) in here else hbm for x in flat],
            out_specs=(vmem,) * len(outs),
            scratch_shapes=buffers + scratch,
            compiler_params=pltpu.CompilerParams(vmem_limit_bytes=limit),
            cost_estimate=pl.CostEstimate(flops=flops, bytes_accessed=min(flops, 1 << 20), transcendentals=0),
            name=name,
        )(*flat)

    here = set()
    tall = (groups * chans, GROUP)
    part_shape = (chans, atom_count)
    unit = 2 * slots * atom_count * chans

    def work(ks):
        return [
            pltpu.VMEM(tall, BF16),
            pltpu.VMEM((len(ks),) + tall, BF16),
            pltpu.VMEM((len(ks),) + tall, F32),
            pltpu.VMEM((chans, chans), F32),
            pltpu.VMEM((chans, chans), F32),
            pltpu.VMEM((2, chans, BLOCK), BF16),
        ]

    near, distant = (0, 1), (2, 3)
    rows = chans // batches
    chunk_rows = -(-3 * rows // 8) * 8
    outs = [
        ((2,) + part_shape, BF16),
        ((batches, chunk_rows, chans), F32),
        (tall, F32),
    ]
    near_parts, near_chunks, near_sum = call(
        edge_kernel,
        near,
        outs,
        [feats, gain_row, w_out, cots[:2], w_src, w_edge, counts, src, dst[:2], edges],
        work(near),
        "near_edges",
        1,
        NEAR_VMEM_BYTES,
    )
    far, far_dst, near_chunks = lax.optimization_barrier((far, far_dst, near_chunks))
    dst = dst + [far_dst, move(far_dst, "graph", 1)]
    cots = cots[:2] + [far, move(far, "graph", 1)]
    far_parts, far_chunks, far_sum = call(
        edge_kernel,
        distant,
        outs,
        [feats, gain_row, w_out, cots[2:], w_src, w_edge, counts, src, dst[2:], edges],
        work(distant),
        "far_edges",
        8 * unit,
        FAR_VMEM_BYTES,
    )
    chunks = near_chunks + far_chunks

    given_far = move(far_parts[1], "graph", 1)
    chunks = reduce_batches(chunks, 1)
    chunks, given_far = lax.optimization_barrier((chunks, given_far))
    far_part = (far_parts[0].astype(F32) + given_far.astype(F32)).astype(BF16)
    arrived = move(far_part, "graph", 2)
    own_part = near_parts[0].astype(F32) + move(near_parts[1], "graph", 1).astype(F32)
    chunks = reduce_batches(chunks, batches.bit_length() - 2)
    chunks, arrived = lax.optimization_barrier((chunks, arrived))
    total = chunks.reshape(chunk_rows, chans)
    total = total + move(total, "graph", 2)

    layer_out, grad_atoms = call(
        atom_kernel,
        (),
        [(feats.shape, BF16)] * 2,
        [feats, gain_row, w_src, w_out, cot, near_sum, far_sum, own_part, arrived],
        [],
        "atoms",
        unit // 8,
        FAR_VMEM_BYTES,
    )

    total, layer_out, grad_atoms = lax.optimization_barrier((total, layer_out, grad_atoms))
    theirs = move(total, "graph", 1)
    here |= {id(total), id(theirs)}
    grads = call(
        weight_kernel,
        (),
        [((rows, chans), F32)] * 3 + [((1, rows), F32)],
        [total, theirs, w_src, gain_row],
        [],
        "weights",
        1,
        FAR_VMEM_BYTES,
    )
    return (
        layer_out.reshape(atoms.shape),
        grad_atoms.reshape(atoms.shape),
        *grads[:3],
        grads[3].reshape(rows),
    )


def solution(mesh):
    in_specs = (
        P("dp", "graph", None, None),
        P(),
        P(),
        P(),
        P(),
        P("dp", "graph", None, None),
        P("dp", "graph", None, None),
        P("dp", None, None),
        P("dp", "graph", None, None, None),
        P("dp", "graph", None, None),
    )
    out_specs = (
        P("dp", "graph", None, None),
        P("dp", "graph", None, None),
        P("dp", None),
        P("dp", None),
        P("dp", None),
        P("dp"),
    )
    return jax.shard_map(body, mesh=mesh, in_specs=in_specs, out_specs=out_specs, check_vma=False)
```

```python
import functools

import jax
import jax.numpy as jnp
from jax import lax
from jax.experimental import pallas as pl
from jax.experimental.pallas import tpu as pltpu
from jax.sharding import PartitionSpec as P

DEG_NORM = 23
GROUP = 256
BLOCK = 1024
F32 = jnp.float32
BF16 = jnp.bfloat16
FAR_VMEM_BYTES = 24 * 1024 * 1024
NEAR_VMEM_BYTES = 56 * 1024 * 1024


def dot(a, b):
    return jnp.dot(a, b, preferred_element_type=F32)


def dot_nt(a, b):
    return lax.dot_general(a, b, (((1,), (1,)), ((), ())), preferred_element_type=F32)


def split(x):
    high = x.astype(BF16)
    return high, (x - high.astype(F32)).astype(BF16)


def stack_groups(x, groups):
    return jnp.concatenate([x[:, g * GROUP : (g + 1) * GROUP] for g in range(groups)], axis=0)


def unstack_groups(x, groups):
    rows = x.shape[0] // groups
    return jnp.concatenate([x[g * rows : (g + 1) * rows, :] for g in range(groups)], axis=1)


def spread(x, which, groups):
    return jnp.concatenate([x * (which == g).astype(F32).astype(BF16) for g in range(groups)], axis=0)


def choose(x, which, groups):
    rows = x.shape[0] // groups
    out = x[:rows, :]
    for g in range(1, groups):
        out = jnp.where(which == g, x[g * rows : (g + 1) * rows, :], out)
    return out


def one_hot(low):
    place = lax.broadcasted_iota(jnp.int32, (GROUP, low.shape[1]), 0)
    return jnp.where(place == low, 1.0, 0.0).astype(BF16)


def column(gain):
    return jnp.broadcast_to(gain[...], (gain.shape[1], gain.shape[1])).T[:, :1]


def norm_parts(atoms):
    feats = atoms.astype(F32).T
    inv = lax.rsqrt(jnp.mean(feats * feats, axis=0, keepdims=True) + 1e-06)
    return feats, inv


def peer_of(k):
    return lax.axis_index("graph") ^ k


class Fetched:
    def __init__(self, source, held, sem):
        self.held = held
        self.copy = pltpu.make_async_copy(source, held, sem)
        self.copy.start()

    def take(self):
        if self.copy is not None:
            self.copy.wait()
            self.copy = None
        return self.held


class Many:
    def __init__(self, moves, held):
        self.held = held
        self.parts = [Fetched(*move) for move in moves]

    def take(self):
        for part in self.parts:
            part.take()
        return self.held


class Held:
    def __init__(self, held):
        self.held = held

    def take(self):
        return self.held


def with_fetches(kernel, kinds, ks, outs, *refs):
    refs = list(refs)
    count = sum(len(ks) if kind in ("many", "each") else 1 for kind in kinds)
    ins, refs = refs[:count], refs[count:]
    results, refs = refs[:outs], refs[outs:]
    given = []
    ins = iter(ins)
    for kind in kinds:
        ref = next(ins)
        if kind == "many":
            held, sems = refs.pop(0), refs.pop(0)
            sources = [ref] + [next(ins) for _ in ks[1:]]
            given.append(Many([(x, held.at[i], sems.at[i]) for i, x in enumerate(sources)], held))
        elif kind == "each":
            given.append(Held([ref] + [next(ins) for _ in ks[1:]]))
        elif kind == "edges":
            held, sems = refs.pop(0), refs.pop(0)
            given.append(Many([(ref.at[peer_of(k)], held.at[i], sems.at[i]) for i, k in enumerate(ks)], held))
        elif kind == "copy":
            given.append(Fetched(ref, refs.pop(0), refs.pop(0)))
        else:
            given.append(Held(ref))
    kernel(ks, *given, *results, *refs)


def back_table(w_out, cot, groups):
    back_t = (dot_nt(w_out[...], cot) * (1.0 / DEG_NORM)).astype(BF16)
    return stack_groups(back_t, groups)


def block_finder(ks, counts):
    sizes = [counts[lax.axis_index("graph"), peer_of(k)] for k in ks]
    firsts = [0]
    for size in sizes:
        firsts.append(firsts[-1] + (size + BLOCK - 1) // BLOCK)

    def locate(item):
        i = jnp.int32(0)
        first = jnp.int32(0)
        peer = peer_of(ks[0])
        size = sizes[0]
        for j in range(1, len(ks)):
            past = item >= firsts[j]
            i = jnp.where(past, j, i)
            first = jnp.where(past, firsts[j], first)
            peer = jnp.where(past, peer_of(ks[j]), peer)
            size = jnp.where(past, sizes[j], size)
        start = pl.multiple_of((item - first) * BLOCK, BLOCK)
        live = lax.broadcasted_iota(jnp.int32, (1, BLOCK), 1) + start < size
        return i, peer, pl.ds(start, BLOCK), live

    return firsts[-1], locate


def low_high(index, live):
    return jnp.where(live, index % GROUP, -1), index // GROUP


def edge_kernel(
    ks,
    atoms,
    gain,
    w_out,
    cots,
    w_src,
    w_edge,
    counts,
    src,
    dsts,
    edges,
    parts,
    chunks,
    dpres,
    table,
    back,
    agg_sum,
    row_sum,
    edge_sum,
    hold,
):
    chans = edge_sum.shape[0]
    groups = back.shape[1] // chans
    agg_sum[...] = jnp.zeros_like(agg_sum)
    row_sum[...] = jnp.zeros_like(row_sum)
    edge_sum[...] = jnp.zeros_like(edge_sum)
    atoms, gain, w_out, cots = atoms.take(), gain.take(), w_out.take(), cots.take()
    cots = [cots[i][...] for i in range(len(ks))]
    w_src_t, w_edge_t = w_src.take()[...].T, w_edge.take()[...].T
    feats, inv = norm_parts(atoms[...])
    table[...] = stack_groups((feats * inv * column(gain)).astype(BF16), groups)
    for i in range(len(ks)):
        back[i] = back_table(w_out, cots[i], groups)
    counts, src, dsts, edges = counts.take(), src.take(), dsts.take(), edges.take()
    whole = edges.shape[0] != len(ks)
    me = lax.axis_index("graph")
    total, locate = block_finder(ks, counts)

    def gather(item):
        i, peer, span, live = locate(item)
        s_low, s_high = low_high(src[pl.ds(peer, 1), span], live)
        d_low, d_high = low_high(dsts[i, pl.ds(me, 1), span], live)
        rows = choose(dot(table[...], one_hot(s_low)), s_high, groups).astype(BF16)
        pre = dot(w_src_t, rows) + dot_nt(w_edge_t, edges[peer if whole else i, span, :])
        slot_back = choose(dot(back[i], one_hot(d_low)), d_high, groups)
        sig = 0.5 * jnp.tanh(0.5 * pre) + 0.5
        act = pre * sig
        slope = sig + act - act * sig
        return rows, act.astype(BF16), (slot_back * slope).astype(BF16)

    def add_up(item, rows, msg):
        i, peer, span, live = locate(item)
        d_low, d_high = low_high(dsts[i, pl.ds(me, 1), span], live)
        dpre = dpres[i, :, span]
        agg_sum[i] += dot_nt(spread(msg, d_high, groups), one_hot(d_low))
        edge_sum[...] += dot(dpre, edges[peer if whole else i, span, :])
        row_sum[...] += dot_nt(rows, dpre)

    def put(item, rows, msg, dpre):
        i, _, span, _ = locate(item)
        hold[0] = rows
        hold[1] = msg
        dpres[i, :, span] = dpre

    def step(item, carry):
        rows, msg = hold[0], hold[1]
        fresh = gather(item)
        add_up(item - 1, rows, msg)
        put(item, *fresh)
        return carry

    @pl.when(total > 0)
    def _():
        put(0, *gather(0))

    lax.fori_loop(1, total, step, 0)

    @pl.when(total > 0)
    def _():
        add_up(total - 1, hold[0], hold[1])

    grad_out = jnp.zeros((chans, chans), F32)
    for i in range(len(ks)):
        part = (unstack_groups(agg_sum[i], groups) * (1.0 / DEG_NORM)).astype(BF16)
        parts[i] = part
        grad_out = grad_out + dot(part, cots[i])
    batches = chunks.shape[0]
    rows = chans // batches
    left = chunks.shape[1] - 3 * rows
    mine = lax.axis_index("dp")
    for n, grad in enumerate((row_sum[...], edge_sum[...].T, grad_out)):
        for j in range(batches):
            chunks[j ^ mine, n * rows : (n + 1) * rows, :] = grad[j * rows : (j + 1) * rows, :]
    if left:
        for j in range(batches):
            chunks[j, 3 * rows :, :] = jnp.zeros((left, chans), F32)


def source_kernel(ks, counts, src, dpres, *refs):
    *before, src_sum = refs
    groups = src_sum.shape[0] // dpres.held.shape[1]
    src_sum[...] = before[0].take()[...] if before else jnp.zeros_like(src_sum)
    counts, src, dpres = counts.take(), src.take(), dpres.take()
    total, locate = block_finder(ks, counts)

    def step(item, carry):
        i, peer, span, live = locate(item)
        s_low, s_high = low_high(src[pl.ds(peer, 1), span], live)
        src_sum[...] += dot_nt(spread(dpres[i, :, span], s_high, groups), one_hot(s_low))
        return carry

    lax.fori_loop(0, total, step, 0)


def atom_kernel(ks, atoms, gain, w_src, w_out, cot, src_sum, agg_a, agg_b, layer_out, grad_atoms):
    feats_rows = atoms.take()[...]
    feats, inv = norm_parts(feats_rows)
    groups = feats_rows.shape[0] // GROUP
    high, low = split(unstack_groups(src_sum.take()[...], groups))
    w_src = w_src.take()[...]
    scaled = column(gain.take()) * (dot(w_src, high) + dot(w_src, low))
    mean = jnp.mean(feats * scaled, axis=0, keepdims=True)
    rest = inv * scaled - feats * (inv * inv * inv * mean)
    grad_atoms[...] = (cot.take()[...].astype(F32) + rest.T).astype(BF16)
    agg = (agg_a.take()[...].astype(F32) + agg_b.take()[...].astype(F32)).T.astype(BF16)
    layer_out[...] = (feats_rows.astype(F32) + dot(agg, w_out.take()[...])).astype(BF16)


def weight_kernel(ks, ours, theirs, w_src, gain, grad_src, grad_edge, grad_out, grad_gain):
    rows, chans = grad_src.shape
    total = ours.take()[...] + theirs.take()[...]
    for n, out in enumerate((grad_src, grad_edge, grad_out)):
        out[...] = total[n * rows : (n + 1) * rows, :]
    place = lax.broadcasted_iota(jnp.int32, (rows, chans), 1)
    row = lax.broadcasted_iota(jnp.int32, (rows, chans), 0)
    mine = place == row + lax.axis_index("dp") * rows
    w_rows = dot(jnp.where(mine, 1.0, 0.0).astype(BF16), w_src.take()[...])
    gains = jnp.sum(jnp.where(mine, gain.take()[...], 0.0), axis=1, keepdims=True)
    value = jnp.sum(w_rows * total[:rows, :], axis=1, keepdims=True) / gains
    grad_gain[...] = jnp.sum(jnp.where(place == row, value, 0.0), axis=0, keepdims=True)[:, :rows]


def move(x, axis, bit):
    size = lax.axis_size(axis)
    return lax.ppermute(x, axis, [(i, i ^ bit) for i in range(size)])


def reduce_batches(chunks, bits):
    for _ in range(bits):
        batches, rows, width = chunks.shape
        bit = lax.axis_size("dp") // batches
        pair = chunks.reshape(batches // 2, 2, rows, width)
        chunks = pair[:, 0] + move(pair[:, 1], "dp", bit)
    return chunks


def body(atoms, gain, w_src, w_edge, w_out, send_src, recv_dst, edge_count, edge_feat, cotangent):
    shards = lax.axis_size("graph")
    batches = lax.axis_size("dp")
    atom_count, chans = atoms.shape[2:]
    slots = send_src.shape[3]
    groups = atom_count // GROUP
    feats = atoms.reshape(atom_count, chans)
    src = send_src.reshape(shards, slots)
    dst_here = recv_dst.reshape(shards, slots)
    cot = cotangent.reshape(atom_count, chans)
    gain_row = gain.reshape(1, chans)
    edges = edge_feat.reshape(shards, slots, edge_feat.shape[4])
    counts = edge_count.reshape(shards, shards)

    far_dst = move(dst_here, "graph", 2)
    far = move(cot, "graph", 2)
    dst = [dst_here, move(dst_here, "graph", 1)]
    cots = [cot, move(cot, "graph", 1), far]

    vmem = pl.BlockSpec(memory_space=pltpu.VMEM)
    hbm = pl.BlockSpec(memory_space=pltpu.HBM)

    def call(kernel, ks, outs, ins, scratch, name, flops, limit, fetch=False):
        kinds, flat, buffers, here = [], [], [], set()
        for x in ins:
            if isinstance(x, list) and not fetch and x[0].dtype == BF16:
                kinds.append("each")
                flat += x
                here.update(id(y) for y in x)
            elif isinstance(x, list):
                kinds.append("many")
                flat += x
                buffers += [pltpu.VMEM((len(x),) + x[0].shape, x[0].dtype), pltpu.SemaphoreType.DMA((len(x),))]
            elif x is edges and fetch:
                kinds.append("edges")
                flat.append(x)
                buffers += [pltpu.VMEM((len(ks),) + x.shape[1:], x.dtype), pltpu.SemaphoreType.DMA((len(ks),))]
            elif x is not counts and not fetch:
                kinds.append("here")
                flat.append(x)
                here.add(id(x))
            else:
                kinds.append("copy")
                flat.append(x)
                space = pltpu.SMEM if x is counts else pltpu.VMEM
                buffers += [space(x.shape, x.dtype), pltpu.SemaphoreType.DMA]
        return pl.pallas_call(
            functools.partial(with_fetches, kernel, kinds, ks, len(outs)),
            out_shape=tuple(jax.ShapeDtypeStruct(shape, kind) for shape, kind in outs),
            in_specs=[vmem if id(x) in here else hbm for x in flat],
            out_specs=(vmem,) * len(outs),
            scratch_shapes=buffers + scratch,
            compiler_params=pltpu.CompilerParams(vmem_limit_bytes=limit),
            cost_estimate=pl.CostEstimate(flops=flops, bytes_accessed=min(flops, 1 << 20), transcendentals=0),
            name=name,
        )(*flat)

    tall = (groups * chans, GROUP)
    part_shape = (chans, atom_count)
    unit = 2 * slots * atom_count * chans

    def work(ks):
        return [
            pltpu.VMEM(tall, BF16),
            pltpu.VMEM((len(ks),) + tall, BF16),
            pltpu.VMEM((len(ks),) + tall, F32),
            pltpu.VMEM((chans, chans), F32),
            pltpu.VMEM((chans, chans), F32),
            pltpu.VMEM((2, chans, BLOCK), BF16),
        ]

    near, distant = (0, 1), (2, 3)
    rows = chans // batches
    chunk_rows = -(-3 * rows // 8) * 8
    outs = [
        ((2,) + part_shape, BF16),
        ((batches, chunk_rows, chans), F32),
        ((2, chans, slots), BF16),
    ]
    near_parts, near_chunks, near_dpre = call(
        edge_kernel,
        near,
        outs,
        [feats, gain_row, w_out, cots[:2], w_src, w_edge, counts, src, dst[:2], edges],
        work(near),
        "near_edges",
        1,
        NEAR_VMEM_BYTES,
        fetch=True,
    )
    far, far_dst, near_chunks = lax.optimization_barrier((far, far_dst, near_chunks))
    dst = dst + [far_dst, move(far_dst, "graph", 1)]
    cots = cots[:2] + [far, move(far, "graph", 1)]
    far_parts, far_chunks, far_dpre = call(
        edge_kernel,
        distant,
        outs,
        [feats, gain_row, w_out, cots[2:], w_src, w_edge, counts, src, dst[2:], edges],
        work(distant),
        "far_edges",
        8 * unit,
        FAR_VMEM_BYTES,
    )
    chunks = near_chunks + far_chunks

    def sum_sources(ks, dpre, before, name):
        (total,) = call(
            source_kernel,
            ks,
            [(tall, F32)],
            [counts, src, dpre] + before,
            [],
            name,
            unit,
            FAR_VMEM_BYTES,
        )
        return total

    given_far = move(far_parts[1], "graph", 1)
    src_sum = sum_sources(near, near_dpre, [], "near_sources")
    given_far, src_sum = lax.optimization_barrier((given_far, src_sum))
    far_part = (far_parts[0].astype(F32) + given_far.astype(F32)).astype(BF16)
    arrived = move(far_part, "graph", 2)
    own_part = near_parts[0].astype(F32) + move(near_parts[1], "graph", 1).astype(F32)
    chunks = reduce_batches(chunks, 1)
    chunks, src_sum, far_dpre = lax.optimization_barrier((chunks, src_sum, far_dpre))
    src_sum = sum_sources(distant, far_dpre, [src_sum], "far_sources")
    chunks = reduce_batches(chunks, 1)
    chunks, src_sum = lax.optimization_barrier((chunks, src_sum))
    chunks = reduce_batches(chunks, batches.bit_length() - 3)
    chunks, arrived = lax.optimization_barrier((chunks, arrived))
    total = chunks.reshape(chunk_rows, chans)
    total = total + move(total, "graph", 2)

    layer_out, grad_atoms = call(
        atom_kernel,
        (),
        [(feats.shape, BF16)] * 2,
        [feats, gain_row, w_src, w_out, cot, src_sum, own_part, arrived],
        [],
        "atoms",
        unit // 8,
        FAR_VMEM_BYTES,
    )

    total, layer_out, grad_atoms = lax.optimization_barrier((total, layer_out, grad_atoms))
    theirs = move(total, "graph", 1)
    grads = call(
        weight_kernel,
        (),
        [((rows, chans), F32)] * 3 + [((1, rows), F32)],
        [total, theirs, w_src, gain_row],
        [],
        "weights",
        1,
        FAR_VMEM_BYTES,
    )
    return (
        layer_out.reshape(atoms.shape),
        grad_atoms.reshape(atoms.shape),
        *grads[:3],
        grads[3].reshape(rows),
    )


def solution(mesh):
    in_specs = (
        P("dp", "graph", None, None),
        P(),
        P(),
        P(),
        P(),
        P("dp", "graph", None, None),
        P("dp", "graph", None, None),
        P("dp", None, None),
        P("dp", "graph", None, None, None),
        P("dp", "graph", None, None),
    )
    out_specs = (
        P("dp", "graph", None, None),
        P("dp", "graph", None, None),
        P("dp", None),
        P("dp", None),
        P("dp", None),
        P("dp"),
    )
    return jax.shard_map(body, mesh=mesh, in_specs=in_specs, out_specs=out_specs, check_vma=False)
```

```python
import functools

import jax
import jax.numpy as jnp
from jax import lax
from jax.experimental import pallas as pl
from jax.experimental.pallas import tpu as pltpu
from jax.sharding import PartitionSpec as P

DEG_NORM = 23
GROUP = 256
BLOCK = 1024
F32 = jnp.float32
BF16 = jnp.bfloat16
FAR_VMEM_BYTES = 24 * 1024 * 1024
NEAR_VMEM_BYTES = 56 * 1024 * 1024


def dot(a, b):
    return jnp.dot(a, b, preferred_element_type=F32)


def dot_nt(a, b):
    return lax.dot_general(a, b, (((1,), (1,)), ((), ())), preferred_element_type=F32)


def split(x):
    high = x.astype(BF16)
    return high, (x - high.astype(F32)).astype(BF16)


def stack_groups(x, groups):
    return jnp.concatenate([x[:, g * GROUP : (g + 1) * GROUP] for g in range(groups)], axis=0)


def unstack_groups(x, groups):
    rows = x.shape[0] // groups
    return jnp.concatenate([x[g * rows : (g + 1) * rows, :] for g in range(groups)], axis=1)


def spread(x, which, groups):
    return jnp.concatenate([x * (which == g).astype(F32).astype(BF16) for g in range(groups)], axis=0)


def choose(x, which, groups):
    rows = x.shape[0] // groups
    out = x[:rows, :]
    for g in range(1, groups):
        out = jnp.where(which == g, x[g * rows : (g + 1) * rows, :], out)
    return out


def one_hot(low):
    place = lax.broadcasted_iota(jnp.int32, (GROUP, low.shape[1]), 0)
    return jnp.where(place == low, 1.0, 0.0).astype(BF16)


def column(gain):
    return jnp.broadcast_to(gain[...], (gain.shape[1], gain.shape[1])).T[:, :1]


def norm_parts(atoms):
    feats = atoms.astype(F32).T
    inv = lax.rsqrt(jnp.mean(feats * feats, axis=0, keepdims=True) + 1e-06)
    return feats, inv


def peer_of(k):
    return lax.axis_index("graph") ^ k


class Fetched:
    def __init__(self, source, held, sem):
        self.held = held
        self.copy = pltpu.make_async_copy(source, held, sem)
        self.copy.start()

    def take(self):
        if self.copy is not None:
            self.copy.wait()
            self.copy = None
        return self.held


class Many:
    def __init__(self, moves, held):
        self.held = held
        self.parts = [Fetched(*move) for move in moves]

    def take(self):
        for part in self.parts:
            part.take()
        return self.held


class Held:
    def __init__(self, held):
        self.held = held

    def take(self):
        return self.held


def with_fetches(kernel, kinds, ks, outs, *refs):
    refs = list(refs)
    count = sum(len(ks) if kind in ("many", "each") else 1 for kind in kinds)
    ins, refs = refs[:count], refs[count:]
    results, refs = refs[:outs], refs[outs:]
    given = []
    ins = iter(ins)
    for kind in kinds:
        ref = next(ins)
        if kind == "many":
            held, sems = refs.pop(0), refs.pop(0)
            sources = [ref] + [next(ins) for _ in ks[1:]]
            given.append(Many([(x, held.at[i], sems.at[i]) for i, x in enumerate(sources)], held))
        elif kind == "each":
            given.append(Held([ref] + [next(ins) for _ in ks[1:]]))
        elif kind == "edges":
            held, sems = refs.pop(0), refs.pop(0)
            given.append(Many([(ref.at[peer_of(k)], held.at[i], sems.at[i]) for i, k in enumerate(ks)], held))
        elif kind == "copy":
            given.append(Fetched(ref, refs.pop(0), refs.pop(0)))
        else:
            given.append(Held(ref))
    kernel(ks, *given, *results, *refs)


def back_table(w_out, cot, groups):
    back_t = (dot_nt(w_out[...], cot) * (1.0 / DEG_NORM)).astype(BF16)
    return stack_groups(back_t, groups)


def block_finder(ks, counts):
    sizes = [counts[lax.axis_index("graph"), peer_of(k)] for k in ks]
    firsts = [0]
    for size in sizes:
        firsts.append(firsts[-1] + (size + BLOCK - 1) // BLOCK)

    def locate(item):
        i = jnp.int32(0)
        first = jnp.int32(0)
        peer = peer_of(ks[0])
        size = sizes[0]
        for j in range(1, len(ks)):
            past = item >= firsts[j]
            i = jnp.where(past, j, i)
            first = jnp.where(past, firsts[j], first)
            peer = jnp.where(past, peer_of(ks[j]), peer)
            size = jnp.where(past, sizes[j], size)
        start = pl.multiple_of((item - first) * BLOCK, BLOCK)
        live = lax.broadcasted_iota(jnp.int32, (1, BLOCK), 1) + start < size
        return i, peer, pl.ds(start, BLOCK), live

    return firsts[-1], locate


def low_high(index, live):
    return jnp.where(live, index % GROUP, -1), index // GROUP


def edge_kernel(
    ks,
    atoms,
    gain,
    w_out,
    cots,
    w_src,
    w_edge,
    counts,
    src,
    dsts,
    edges,
    part_a,
    part_b,
    chunks,
    dpres,
    table,
    back,
    agg_sum,
    row_sum,
    edge_sum,
    hold,
):
    chans = edge_sum.shape[0]
    groups = back.shape[1] // chans
    agg_sum[...] = jnp.zeros_like(agg_sum)
    row_sum[...] = jnp.zeros_like(row_sum)
    edge_sum[...] = jnp.zeros_like(edge_sum)
    atoms, gain, w_out, cots = atoms.take(), gain.take(), w_out.take(), cots.take()
    cots = [cots[i][...] for i in range(len(ks))]
    w_src_t, w_edge_t = w_src.take()[...].T, w_edge.take()[...].T
    feats, inv = norm_parts(atoms[...])
    table[...] = stack_groups((feats * inv * column(gain)).astype(BF16), groups)
    for i in range(len(ks)):
        back[i] = back_table(w_out, cots[i], groups)
    counts, src, dsts, edges = counts.take(), src.take(), dsts.take(), edges.take()
    whole = edges.shape[0] != len(ks)
    me = lax.axis_index("graph")
    total, locate = block_finder(ks, counts)

    def gather(item):
        i, peer, span, live = locate(item)
        s_low, s_high = low_high(src[pl.ds(peer, 1), span], live)
        d_low, d_high = low_high(dsts[i, pl.ds(me, 1), span], live)
        rows = choose(dot(table[...], one_hot(s_low)), s_high, groups).astype(BF16)
        pre = dot(w_src_t, rows) + dot_nt(w_edge_t, edges[peer if whole else i, span, :])
        slot_back = choose(dot(back[i], one_hot(d_low)), d_high, groups)
        sig = 0.5 * jnp.tanh(0.5 * pre) + 0.5
        act = pre * sig
        slope = sig + act - act * sig
        return rows, act.astype(BF16), (slot_back * slope).astype(BF16)

    def add_up(item, rows, msg):
        i, peer, span, live = locate(item)
        d_low, d_high = low_high(dsts[i, pl.ds(me, 1), span], live)
        dpre = dpres[i, :, span]
        agg_sum[i] += dot_nt(spread(msg, d_high, groups), one_hot(d_low))
        edge_sum[...] += dot(dpre, edges[peer if whole else i, span, :])
        row_sum[...] += dot_nt(rows, dpre)

    def put(item, rows, msg, dpre):
        i, _, span, _ = locate(item)
        hold[0] = rows
        hold[1] = msg
        dpres[i, :, span] = dpre

    def step(item, carry):
        rows, msg = hold[0], hold[1]
        fresh = gather(item)
        add_up(item - 1, rows, msg)
        put(item, *fresh)
        return carry

    @pl.when(total > 0)
    def _():
        put(0, *gather(0))

    lax.fori_loop(1, total, step, 0)

    @pl.when(total > 0)
    def _():
        add_up(total - 1, hold[0], hold[1])

    grad_out = jnp.zeros((chans, chans), F32)
    for i in range(len(ks)):
        part = (unstack_groups(agg_sum[i], groups) * (1.0 / DEG_NORM)).astype(BF16)
        (part_a, part_b)[i][...] = part
        grad_out = grad_out + dot(part, cots[i])
    batches = chunks.shape[0]
    rows = chans // batches
    left = chunks.shape[1] - 3 * rows
    mine = lax.axis_index("dp")
    for n, grad in enumerate((row_sum[...], edge_sum[...].T, grad_out)):
        for j in range(batches):
            chunks[j ^ mine, n * rows : (n + 1) * rows, :] = grad[j * rows : (j + 1) * rows, :]
    if left:
        for j in range(batches):
            chunks[j, 3 * rows :, :] = jnp.zeros((left, chans), F32)


def source_kernel(ks, counts, src, dpres, *refs):
    *before, src_sum = refs
    groups = src_sum.shape[0] // dpres.held.shape[1]
    src_sum[...] = before[0].take()[...] if before else jnp.zeros_like(src_sum)
    counts, src, dpres = counts.take(), src.take(), dpres.take()
    total, locate = block_finder(ks, counts)

    def step(item, carry):
        i, peer, span, live = locate(item)
        s_low, s_high = low_high(src[pl.ds(peer, 1), span], live)
        src_sum[...] += dot_nt(spread(dpres[i, :, span], s_high, groups), one_hot(s_low))
        return carry

    lax.fori_loop(0, total, step, 0)


def atom_kernel(ks, atoms, gain, w_src, w_out, cot, src_sum, agg_a, agg_b, layer_out, grad_atoms):
    feats_rows = atoms.take()[...]
    feats, inv = norm_parts(feats_rows)
    groups = feats_rows.shape[0] // GROUP
    high, low = split(unstack_groups(src_sum.take()[...], groups))
    w_src = w_src.take()[...]
    scaled = column(gain.take()) * (dot(w_src, high) + dot(w_src, low))
    mean = jnp.mean(feats * scaled, axis=0, keepdims=True)
    rest = inv * scaled - feats * (inv * inv * inv * mean)
    grad_atoms[...] = (cot.take()[...].astype(F32) + rest.T).astype(BF16)
    agg = (agg_a.take()[...].astype(F32) + agg_b.take()[...].astype(F32)).T.astype(BF16)
    layer_out[...] = (feats_rows.astype(F32) + dot(agg, w_out.take()[...])).astype(BF16)


def weight_kernel(ks, ours, theirs, w_src, gain, grad_src, grad_edge, grad_out, grad_gain):
    rows, chans = grad_src.shape
    total = ours.take()[...] + theirs.take()[...]
    for n, out in enumerate((grad_src, grad_edge, grad_out)):
        out[...] = total[n * rows : (n + 1) * rows, :]
    place = lax.broadcasted_iota(jnp.int32, (rows, chans), 1)
    row = lax.broadcasted_iota(jnp.int32, (rows, chans), 0)
    mine = place == row + lax.axis_index("dp") * rows
    w_rows = dot(jnp.where(mine, 1.0, 0.0).astype(BF16), w_src.take()[...])
    gains = jnp.sum(jnp.where(mine, gain.take()[...], 0.0), axis=1, keepdims=True)
    value = jnp.sum(w_rows * total[:rows, :], axis=1, keepdims=True) / gains
    grad_gain[...] = jnp.sum(jnp.where(place == row, value, 0.0), axis=0, keepdims=True)[:, :rows]


def move(x, axis, bit):
    size = lax.axis_size(axis)
    return lax.ppermute(x, axis, [(i, i ^ bit) for i in range(size)])


def reduce_batches(chunks, bits):
    for _ in range(bits):
        batches, rows, width = chunks.shape
        bit = lax.axis_size("dp") // batches
        pair = chunks.reshape(batches // 2, 2, rows, width)
        chunks = pair[:, 0] + move(pair[:, 1], "dp", bit)
    return chunks


def body(atoms, gain, w_src, w_edge, w_out, send_src, recv_dst, edge_count, edge_feat, cotangent):
    shards = lax.axis_size("graph")
    batches = lax.axis_size("dp")
    atom_count, chans = atoms.shape[2:]
    slots = send_src.shape[3]
    groups = atom_count // GROUP
    feats = atoms.reshape(atom_count, chans)
    src = send_src.reshape(shards, slots)
    dst_here = recv_dst.reshape(shards, slots)
    cot = cotangent.reshape(atom_count, chans)
    gain_row = gain.reshape(1, chans)
    edges = edge_feat.reshape(shards, slots, edge_feat.shape[4])
    counts = edge_count.reshape(shards, shards)

    far_dst = move(dst_here, "graph", 2)
    far = move(cot, "graph", 2)
    dst = [dst_here, move(dst_here, "graph", 1)]
    cots = [cot, move(cot, "graph", 1), far]

    vmem = pl.BlockSpec(memory_space=pltpu.VMEM)
    hbm = pl.BlockSpec(memory_space=pltpu.HBM)

    def call(kernel, ks, outs, ins, scratch, name, flops, limit, fetch=False):
        kinds, flat, buffers, here = [], [], [], set()
        for x in ins:
            if isinstance(x, list) and not fetch and x[0].dtype == BF16:
                kinds.append("each")
                flat += x
                here.update(id(y) for y in x)
            elif isinstance(x, list):
                kinds.append("many")
                flat += x
                buffers += [pltpu.VMEM((len(x),) + x[0].shape, x[0].dtype), pltpu.SemaphoreType.DMA((len(x),))]
            elif x is edges and fetch:
                kinds.append("edges")
                flat.append(x)
                buffers += [pltpu.VMEM((len(ks),) + x.shape[1:], x.dtype), pltpu.SemaphoreType.DMA((len(ks),))]
            elif x is not counts and not fetch:
                kinds.append("here")
                flat.append(x)
                here.add(id(x))
            else:
                kinds.append("copy")
                flat.append(x)
                space = pltpu.SMEM if x is counts else pltpu.VMEM
                buffers += [space(x.shape, x.dtype), pltpu.SemaphoreType.DMA]
        return pl.pallas_call(
            functools.partial(with_fetches, kernel, kinds, ks, len(outs)),
            out_shape=tuple(jax.ShapeDtypeStruct(shape, kind) for shape, kind in outs),
            in_specs=[vmem if id(x) in here else hbm for x in flat],
            out_specs=(vmem,) * len(outs),
            scratch_shapes=buffers + scratch,
            compiler_params=pltpu.CompilerParams(vmem_limit_bytes=limit),
            cost_estimate=pl.CostEstimate(flops=flops, bytes_accessed=min(flops, 1 << 20), transcendentals=0),
            name=name,
        )(*flat)

    tall = (groups * chans, GROUP)
    part_shape = (chans, atom_count)
    unit = 2 * slots * atom_count * chans

    def work(ks):
        return [
            pltpu.VMEM(tall, BF16),
            pltpu.VMEM((len(ks),) + tall, BF16),
            pltpu.VMEM((len(ks),) + tall, F32),
            pltpu.VMEM((chans, chans), F32),
            pltpu.VMEM((chans, chans), F32),
            pltpu.VMEM((2, chans, BLOCK), BF16),
        ]

    near, distant = (0, 1), (2, 3)
    rows = chans // batches
    chunk_rows = -(-3 * rows // 8) * 8
    outs = [
        (part_shape, BF16),
        (part_shape, BF16),
        ((batches, chunk_rows, chans), F32),
        ((2, chans, slots), BF16),
    ]
    *near_parts, near_chunks, near_dpre = call(
        edge_kernel,
        near,
        outs,
        [feats, gain_row, w_out, cots[:2], w_src, w_edge, counts, src, dst[:2], edges],
        work(near),
        "near_edges",
        1,
        NEAR_VMEM_BYTES,
        fetch=True,
    )
    far, far_dst, near_chunks = lax.optimization_barrier((far, far_dst, near_chunks))
    dst = dst + [far_dst, move(far_dst, "graph", 1)]
    cots = cots[:2] + [far, move(far, "graph", 1)]
    *far_parts, far_chunks, far_dpre = call(
        edge_kernel,
        distant,
        outs,
        [feats, gain_row, w_out, cots[2:], w_src, w_edge, counts, src, dst[2:], edges],
        work(distant),
        "far_edges",
        8 * unit,
        FAR_VMEM_BYTES,
    )
    chunks = near_chunks + far_chunks

    def sum_sources(ks, dpre, before, name):
        (total,) = call(
            source_kernel,
            ks,
            [(tall, F32)],
            [counts, src, dpre] + before,
            [],
            name,
            unit,
            FAR_VMEM_BYTES,
        )
        return total

    given_far = move(far_parts[1], "graph", 1)
    src_sum = sum_sources(near, near_dpre, [], "near_sources")
    given_far, src_sum = lax.optimization_barrier((given_far, src_sum))
    far_part = (far_parts[0].astype(F32) + given_far.astype(F32)).astype(BF16)
    arrived = move(far_part, "graph", 2)
    own_part = near_parts[0].astype(F32) + move(near_parts[1], "graph", 1).astype(F32)
    chunks = reduce_batches(chunks, 1)
    chunks, src_sum, far_dpre = lax.optimization_barrier((chunks, src_sum, far_dpre))
    src_sum = sum_sources(distant, far_dpre, [src_sum], "far_sources")
    chunks = reduce_batches(chunks, 1)
    chunks, src_sum = lax.optimization_barrier((chunks, src_sum))
    chunks = reduce_batches(chunks, batches.bit_length() - 3)
    chunks, arrived = lax.optimization_barrier((chunks, arrived))
    total = chunks.reshape(chunk_rows, chans)
    total = total + move(total, "graph", 2)

    layer_out, grad_atoms = call(
        atom_kernel,
        (),
        [(feats.shape, BF16)] * 2,
        [feats, gain_row, w_src, w_out, cot, src_sum, own_part, arrived],
        [],
        "atoms",
        unit // 8,
        FAR_VMEM_BYTES,
    )

    total, layer_out, grad_atoms = lax.optimization_barrier((total, layer_out, grad_atoms))
    theirs = move(total, "graph", 1)
    grads = call(
        weight_kernel,
        (),
        [((rows, chans), F32)] * 3 + [((1, rows), F32)],
        [total, theirs, w_src, gain_row],
        [],
        "weights",
        1,
        FAR_VMEM_BYTES,
    )
    return (
        layer_out.reshape(atoms.shape),
        grad_atoms.reshape(atoms.shape),
        *grads[:3],
        grads[3].reshape(rows),
    )


def solution(mesh):
    in_specs = (
        P("dp", "graph", None, None),
        P(),
        P(),
        P(),
        P(),
        P("dp", "graph", None, None),
        P("dp", "graph", None, None),
        P("dp", None, None),
        P("dp", "graph", None, None, None),
        P("dp", "graph", None, None),
    )
    out_specs = (
        P("dp", "graph", None, None),
        P("dp", "graph", None, None),
        P("dp", None),
        P("dp", None),
        P("dp", None),
        P("dp"),
    )
    return jax.shard_map(body, mesh=mesh, in_specs=in_specs, out_specs=out_specs, check_vma=False)
```

```python
import functools

import jax
import jax.numpy as jnp
from jax import lax
from jax.experimental import pallas as pl
from jax.experimental.pallas import tpu as pltpu
from jax.sharding import PartitionSpec as P

DEG_NORM = 23
GROUP = 256
BLOCK = 1024
F32 = jnp.float32
BF16 = jnp.bfloat16
FAR_VMEM_BYTES = 24 * 1024 * 1024
NEAR_VMEM_BYTES = 56 * 1024 * 1024


def dot(a, b):
    return jnp.dot(a, b, preferred_element_type=F32)


def dot_nt(a, b):
    return lax.dot_general(a, b, (((1,), (1,)), ((), ())), preferred_element_type=F32)


def split(x):
    high = x.astype(BF16)
    return high, (x - high.astype(F32)).astype(BF16)


def stack_groups(x, groups):
    return jnp.concatenate([x[:, g * GROUP : (g + 1) * GROUP] for g in range(groups)], axis=0)


def unstack_groups(x, groups):
    rows = x.shape[0] // groups
    return jnp.concatenate([x[g * rows : (g + 1) * rows, :] for g in range(groups)], axis=1)


def spread(x, which, groups):
    return jnp.concatenate([x * (which == g).astype(F32).astype(BF16) for g in range(groups)], axis=0)


def choose(x, which, groups):
    rows = x.shape[0] // groups
    out = x[:rows, :]
    for g in range(1, groups):
        out = jnp.where(which == g, x[g * rows : (g + 1) * rows, :], out)
    return out


def one_hot(low):
    place = lax.broadcasted_iota(jnp.int32, (GROUP, low.shape[1]), 0)
    return jnp.where(place == low, 1.0, 0.0).astype(BF16)


def column(gain):
    return jnp.broadcast_to(gain[...], (gain.shape[1], gain.shape[1])).T[:, :1]


def norm_parts(atoms):
    feats = atoms.astype(F32).T
    inv = lax.rsqrt(jnp.mean(feats * feats, axis=0, keepdims=True) + 1e-06)
    return feats, inv


def peer_of(k):
    return lax.axis_index("graph") ^ k


class Fetched:
    def __init__(self, source, held, sem):
        self.held = held
        self.copy = pltpu.make_async_copy(source, held, sem)
        self.copy.start()

    def take(self):
        if self.copy is not None:
            self.copy.wait()
            self.copy = None
        return self.held


class Many:
    def __init__(self, moves, held):
        self.held = held
        self.parts = [Fetched(*move) for move in moves]

    def take(self):
        for part in self.parts:
            part.take()
        return self.held

    def take_first(self):
        self.parts[0].take()
        return self.held


class Held:
    def __init__(self, held):
        self.held = held

    def take(self):
        return self.held

    def take_first(self):
        return self.held


def with_fetches(kernel, kinds, ks, outs, *refs):
    refs = list(refs)
    count = sum(len(ks) if kind in ("many", "each") else 1 for kind in kinds)
    ins, refs = refs[:count], refs[count:]
    results, refs = refs[:outs], refs[outs:]
    given = []
    ins = iter(ins)
    for kind in kinds:
        ref = next(ins)
        if kind == "many":
            held, sems = refs.pop(0), refs.pop(0)
            sources = [ref] + [next(ins) for _ in ks[1:]]
            given.append(Many([(x, held.at[i], sems.at[i]) for i, x in enumerate(sources)], held))
        elif kind == "each":
            given.append(Held([ref] + [next(ins) for _ in ks[1:]]))
        elif kind == "edges":
            held, sems = refs.pop(0), refs.pop(0)
            given.append(Many([(ref.at[peer_of(k)], held.at[i], sems.at[i]) for i, k in enumerate(ks)], held))
        elif kind == "copy":
            given.append(Fetched(ref, refs.pop(0), refs.pop(0)))
        else:
            given.append(Held(ref))
    kernel(ks, *given, *results, *refs)


def back_table(w_out, cot, groups):
    back_t = (dot_nt(w_out[...], cot) * (1.0 / DEG_NORM)).astype(BF16)
    return stack_groups(back_t, groups)


def block_finder(ks, counts):
    sizes = [counts[lax.axis_index("graph"), peer_of(k)] for k in ks]
    firsts = [0]
    for size in sizes:
        firsts.append(firsts[-1] + (size + BLOCK - 1) // BLOCK)

    def locate(item):
        i = jnp.int32(0)
        first = jnp.int32(0)
        peer = peer_of(ks[0])
        size = sizes[0]
        for j in range(1, len(ks)):
            past = item >= firsts[j]
            i = jnp.where(past, j, i)
            first = jnp.where(past, firsts[j], first)
            peer = jnp.where(past, peer_of(ks[j]), peer)
            size = jnp.where(past, sizes[j], size)
        start = pl.multiple_of((item - first) * BLOCK, BLOCK)
        live = lax.broadcasted_iota(jnp.int32, (1, BLOCK), 1) + start < size
        return i, peer, pl.ds(start, BLOCK), live

    return firsts[-1], locate


def low_high(index, live):
    return jnp.where(live, index % GROUP, -1), index // GROUP


def edge_kernel(
    ks,
    atoms,
    gain,
    w_out,
    cots,
    w_src,
    w_edge,
    counts,
    src,
    dsts,
    edges,
    part_a,
    part_b,
    chunks,
    dpres,
    table,
    back,
    agg_sum,
    row_sum,
    edge_sum,
    hold,
):
    chans = edge_sum.shape[0]
    groups = back.shape[1] // chans
    agg_sum[...] = jnp.zeros_like(agg_sum)
    row_sum[...] = jnp.zeros_like(row_sum)
    edge_sum[...] = jnp.zeros_like(edge_sum)
    atoms, gain, w_out = atoms.take(), gain.take(), w_out.take()
    first_cot = cots.take_first()[0][...]
    w_src_t, w_edge_t = w_src.take()[...].T, w_edge.take()[...].T
    feats, inv = norm_parts(atoms[...])
    table[...] = stack_groups((feats * inv * column(gain)).astype(BF16), groups)
    back[0] = back_table(w_out, first_cot, groups)
    counts, src = counts.take(), src.take()
    late_dsts, late_edges = dsts, edges
    dsts, edges = dsts.take_first(), edges.take_first()
    whole = edges.shape[0] != len(ks)
    ready = isinstance(late_edges, Held)

    def take_rest():
        late_dsts.take()
        late_edges.take()
        held_cots = cots.take()
        for i in range(1, len(ks)):
            back[i] = back_table(w_out, held_cots[i][...], groups)

    if ready:
        take_rest()
    me = lax.axis_index("graph")
    total, locate = block_finder(ks, counts)

    def gather(item):
        i, peer, span, live = locate(item)
        s_low, s_high = low_high(src[pl.ds(peer, 1), span], live)
        d_low, d_high = low_high(dsts[i, pl.ds(me, 1), span], live)
        rows = choose(dot(table[...], one_hot(s_low)), s_high, groups).astype(BF16)
        pre = dot(w_src_t, rows) + dot_nt(w_edge_t, edges[peer if whole else i, span, :])
        slot_back = choose(dot(back[i], one_hot(d_low)), d_high, groups)
        sig = 0.5 * jnp.tanh(0.5 * pre) + 0.5
        act = pre * sig
        slope = sig + act - act * sig
        return rows, act.astype(BF16), (slot_back * slope).astype(BF16)

    def add_up(item, rows, msg):
        i, peer, span, live = locate(item)
        d_low, d_high = low_high(dsts[i, pl.ds(me, 1), span], live)
        dpre = dpres[i, :, span]
        agg_sum[i] += dot_nt(spread(msg, d_high, groups), one_hot(d_low))
        edge_sum[...] += dot(dpre, edges[peer if whole else i, span, :])
        row_sum[...] += dot_nt(rows, dpre)

    def put(item, rows, msg, dpre):
        i, _, span, _ = locate(item)
        hold[0] = rows
        hold[1] = msg
        dpres[i, :, span] = dpre

    def step(item, carry):
        rows, msg = hold[0], hold[1]
        fresh = gather(item)
        add_up(item - 1, rows, msg)
        put(item, *fresh)
        return carry

    @pl.when(total > 0)
    def _():
        put(0, *gather(0))

    if not ready:
        take_rest()

    lax.fori_loop(1, total, step, 0)

    @pl.when(total > 0)
    def _():
        add_up(total - 1, hold[0], hold[1])

    grad_out = jnp.zeros((chans, chans), F32)
    for i in range(len(ks)):
        part = (unstack_groups(agg_sum[i], groups) * (1.0 / DEG_NORM)).astype(BF16)
        (part_a, part_b)[i][...] = part
        grad_out = grad_out + dot(part, cots.take()[i][...])
    batches = chunks.shape[0]
    rows = chans // batches
    left = chunks.shape[1] - 3 * rows
    mine = lax.axis_index("dp")
    for n, grad in enumerate((row_sum[...], edge_sum[...].T, grad_out)):
        for j in range(batches):
            chunks[j ^ mine, n * rows : (n + 1) * rows, :] = grad[j * rows : (j + 1) * rows, :]
    if left:
        for j in range(batches):
            chunks[j, 3 * rows :, :] = jnp.zeros((left, chans), F32)


def source_kernel(ks, counts, src, dpres, *refs):
    *before, src_sum = refs
    groups = src_sum.shape[0] // dpres.held.shape[1]
    src_sum[...] = before[0].take()[...] if before else jnp.zeros_like(src_sum)
    counts, src, dpres = counts.take(), src.take(), dpres.take()
    total, locate = block_finder(ks, counts)

    def step(item, carry):
        i, peer, span, live = locate(item)
        s_low, s_high = low_high(src[pl.ds(peer, 1), span], live)
        src_sum[...] += dot_nt(spread(dpres[i, :, span], s_high, groups), one_hot(s_low))
        return carry

    lax.fori_loop(0, total, step, 0)


def atom_kernel(ks, atoms, gain, w_src, w_out, cot, src_sum, agg_a, agg_b, layer_out, grad_atoms):
    feats_rows = atoms.take()[...]
    feats, inv = norm_parts(feats_rows)
    groups = feats_rows.shape[0] // GROUP
    high, low = split(unstack_groups(src_sum.take()[...], groups))
    w_src = w_src.take()[...]
    scaled = column(gain.take()) * (dot(w_src, high) + dot(w_src, low))
    mean = jnp.mean(feats * scaled, axis=0, keepdims=True)
    rest = inv * scaled - feats * (inv * inv * inv * mean)
    grad_atoms[...] = (cot.take()[...].astype(F32) + rest.T).astype(BF16)
    agg = (agg_a.take()[...].astype(F32) + agg_b.take()[...].astype(F32)).T.astype(BF16)
    layer_out[...] = (feats_rows.astype(F32) + dot(agg, w_out.take()[...])).astype(BF16)


def weight_kernel(ks, ours, theirs, w_src, gain, grad_src, grad_edge, grad_out, grad_gain):
    rows, chans = grad_src.shape
    total = ours.take()[...] + theirs.take()[...]
    for n, out in enumerate((grad_src, grad_edge, grad_out)):
        out[...] = total[n * rows : (n + 1) * rows, :]
    place = lax.broadcasted_iota(jnp.int32, (rows, chans), 1)
    row = lax.broadcasted_iota(jnp.int32, (rows, chans), 0)
    mine = place == row + lax.axis_index("dp") * rows
    w_rows = dot(jnp.where(mine, 1.0, 0.0).astype(BF16), w_src.take()[...])
    gains = jnp.sum(jnp.where(mine, gain.take()[...], 0.0), axis=1, keepdims=True)
    value = jnp.sum(w_rows * total[:rows, :], axis=1, keepdims=True) / gains
    grad_gain[...] = jnp.sum(jnp.where(place == row, value, 0.0), axis=0, keepdims=True)[:, :rows]


def move(x, axis, bit):
    size = lax.axis_size(axis)
    return lax.ppermute(x, axis, [(i, i ^ bit) for i in range(size)])


def reduce_batches(chunks, bits):
    for _ in range(bits):
        batches, rows, width = chunks.shape
        bit = lax.axis_size("dp") // batches
        pair = chunks.reshape(batches // 2, 2, rows, width)
        chunks = pair[:, 0] + move(pair[:, 1], "dp", bit)
    return chunks


def body(atoms, gain, w_src, w_edge, w_out, send_src, recv_dst, edge_count, edge_feat, cotangent):
    shards = lax.axis_size("graph")
    batches = lax.axis_size("dp")
    atom_count, chans = atoms.shape[2:]
    slots = send_src.shape[3]
    groups = atom_count // GROUP
    feats = atoms.reshape(atom_count, chans)
    src = send_src.reshape(shards, slots)
    dst_here = recv_dst.reshape(shards, slots)
    cot = cotangent.reshape(atom_count, chans)
    gain_row = gain.reshape(1, chans)
    edges = edge_feat.reshape(shards, slots, edge_feat.shape[4])
    counts = edge_count.reshape(shards, shards)

    far_dst = move(dst_here, "graph", 2)
    far = move(cot, "graph", 2)
    dst = [dst_here, move(dst_here, "graph", 1)]
    cots = [cot, move(cot, "graph", 1), far]

    vmem = pl.BlockSpec(memory_space=pltpu.VMEM)
    hbm = pl.BlockSpec(memory_space=pltpu.HBM)

    def call(kernel, ks, outs, ins, scratch, name, flops, limit, fetch=False):
        kinds, flat, buffers, here = [], [], [], set()
        for x in ins:
            if isinstance(x, list) and not fetch and x[0].dtype == BF16:
                kinds.append("each")
                flat += x
                here.update(id(y) for y in x)
            elif isinstance(x, list):
                kinds.append("many")
                flat += x
                buffers += [pltpu.VMEM((len(x),) + x[0].shape, x[0].dtype), pltpu.SemaphoreType.DMA((len(x),))]
            elif x is edges and fetch:
                kinds.append("edges")
                flat.append(x)
                buffers += [pltpu.VMEM((len(ks),) + x.shape[1:], x.dtype), pltpu.SemaphoreType.DMA((len(ks),))]
            elif x is not counts and not fetch:
                kinds.append("here")
                flat.append(x)
                here.add(id(x))
            else:
                kinds.append("copy")
                flat.append(x)
                space = pltpu.SMEM if x is counts else pltpu.VMEM
                buffers += [space(x.shape, x.dtype), pltpu.SemaphoreType.DMA]
        return pl.pallas_call(
            functools.partial(with_fetches, kernel, kinds, ks, len(outs)),
            out_shape=tuple(jax.ShapeDtypeStruct(shape, kind) for shape, kind in outs),
            in_specs=[vmem if id(x) in here else hbm for x in flat],
            out_specs=(vmem,) * len(outs),
            scratch_shapes=buffers + scratch,
            compiler_params=pltpu.CompilerParams(vmem_limit_bytes=limit),
            cost_estimate=pl.CostEstimate(flops=flops, bytes_accessed=min(flops, 1 << 20), transcendentals=0),
            name=name,
        )(*flat)

    tall = (groups * chans, GROUP)
    part_shape = (chans, atom_count)
    unit = 2 * slots * atom_count * chans

    def work(ks):
        return [
            pltpu.VMEM(tall, BF16),
            pltpu.VMEM((len(ks),) + tall, BF16),
            pltpu.VMEM((len(ks),) + tall, F32),
            pltpu.VMEM((chans, chans), F32),
            pltpu.VMEM((chans, chans), F32),
            pltpu.VMEM((2, chans, BLOCK), BF16),
        ]

    near, distant = (0, 1), (2, 3)
    rows = chans // batches
    chunk_rows = -(-3 * rows // 8) * 8
    outs = [
        (part_shape, BF16),
        (part_shape, BF16),
        ((batches, chunk_rows, chans), F32),
        ((2, chans, slots), BF16),
    ]
    *near_parts, near_chunks, near_dpre = call(
        edge_kernel,
        near,
        outs,
        [feats, gain_row, w_out, cots[:2], w_src, w_edge, counts, src, dst[:2], edges],
        work(near),
        "near_edges",
        1,
        NEAR_VMEM_BYTES,
        fetch=True,
    )
    far, far_dst, near_chunks = lax.optimization_barrier((far, far_dst, near_chunks))
    dst = dst + [far_dst, move(far_dst, "graph", 1)]
    cots = cots[:2] + [far, move(far, "graph", 1)]
    *far_parts, far_chunks, far_dpre = call(
        edge_kernel,
        distant,
        outs,
        [feats, gain_row, w_out, cots[2:], w_src, w_edge, counts, src, dst[2:], edges],
        work(distant),
        "far_edges",
        8 * unit,
        FAR_VMEM_BYTES,
    )
    chunks = near_chunks + far_chunks

    def sum_sources(ks, dpre, before, name):
        (total,) = call(
            source_kernel,
            ks,
            [(tall, F32)],
            [counts, src, dpre] + before,
            [],
            name,
            unit,
            FAR_VMEM_BYTES,
        )
        return total

    given_far = move(far_parts[1], "graph", 1)
    src_sum = sum_sources(near, near_dpre, [], "near_sources")
    given_far, src_sum = lax.optimization_barrier((given_far, src_sum))
    far_part = (far_parts[0].astype(F32) + given_far.astype(F32)).astype(BF16)
    arrived = move(far_part, "graph", 2)
    own_part = near_parts[0].astype(F32) + move(near_parts[1], "graph", 1).astype(F32)
    chunks = reduce_batches(chunks, 1)
    chunks, src_sum, far_dpre = lax.optimization_barrier((chunks, src_sum, far_dpre))
    src_sum = sum_sources(distant, far_dpre, [src_sum], "far_sources")
    chunks = reduce_batches(chunks, 1)
    chunks, src_sum = lax.optimization_barrier((chunks, src_sum))
    chunks = reduce_batches(chunks, batches.bit_length() - 3)
    chunks, arrived = lax.optimization_barrier((chunks, arrived))
    total = chunks.reshape(chunk_rows, chans)
    total = total + move(total, "graph", 2)

    layer_out, grad_atoms = call(
        atom_kernel,
        (),
        [(feats.shape, BF16)] * 2,
        [feats, gain_row, w_src, w_out, cot, src_sum, own_part, arrived],
        [],
        "atoms",
        unit // 8,
        FAR_VMEM_BYTES,
    )

    total, layer_out, grad_atoms = lax.optimization_barrier((total, layer_out, grad_atoms))
    theirs = move(total, "graph", 1)
    grads = call(
        weight_kernel,
        (),
        [((rows, chans), F32)] * 3 + [((1, rows), F32)],
        [total, theirs, w_src, gain_row],
        [],
        "weights",
        1,
        FAR_VMEM_BYTES,
    )
    return (
        layer_out.reshape(atoms.shape),
        grad_atoms.reshape(atoms.shape),
        *grads[:3],
        grads[3].reshape(rows),
    )


def solution(mesh):
    in_specs = (
        P("dp", "graph", None, None),
        P(),
        P(),
        P(),
        P(),
        P("dp", "graph", None, None),
        P("dp", "graph", None, None),
        P("dp", None, None),
        P("dp", "graph", None, None, None),
        P("dp", "graph", None, None),
    )
    out_specs = (
        P("dp", "graph", None, None),
        P("dp", "graph", None, None),
        P("dp", None),
        P("dp", None),
        P("dp", None),
        P("dp"),
    )
    return jax.shard_map(body, mesh=mesh, in_specs=in_specs, out_specs=out_specs, check_vma=False)
```

```python
import functools

import jax
import jax.numpy as jnp
from jax import lax
from jax.experimental import pallas as pl
from jax.experimental.pallas import tpu as pltpu
from jax.sharding import PartitionSpec as P

DEG_NORM = 23
GROUP = 256
BLOCK = 1024
F32 = jnp.float32
BF16 = jnp.bfloat16
FAR_VMEM_BYTES = 24 * 1024 * 1024
NEAR_VMEM_BYTES = 56 * 1024 * 1024


def dot(a, b):
    return jnp.dot(a, b, preferred_element_type=F32)


def dot_nt(a, b):
    return lax.dot_general(a, b, (((1,), (1,)), ((), ())), preferred_element_type=F32)


def split(x):
    high = x.astype(BF16)
    return high, (x - high.astype(F32)).astype(BF16)


def stack_groups(x, groups):
    return jnp.concatenate([x[:, g * GROUP : (g + 1) * GROUP] for g in range(groups)], axis=0)


def unstack_groups(x, groups):
    rows = x.shape[0] // groups
    return jnp.concatenate([x[g * rows : (g + 1) * rows, :] for g in range(groups)], axis=1)


def spread(x, which, groups):
    return jnp.concatenate([x * (which == g).astype(F32).astype(BF16) for g in range(groups)], axis=0)


def choose(x, which, groups):
    rows = x.shape[0] // groups
    out = x[:rows, :]
    for g in range(1, groups):
        out = jnp.where(which == g, x[g * rows : (g + 1) * rows, :], out)
    return out


def one_hot(low):
    place = lax.broadcasted_iota(jnp.int32, (GROUP, low.shape[1]), 0)
    return jnp.where(place == low, 1.0, 0.0).astype(BF16)


def column(gain):
    return jnp.broadcast_to(gain[...], (gain.shape[1], gain.shape[1])).T[:, :1]


def norm_parts(atoms):
    feats = atoms.astype(F32).T
    inv = lax.rsqrt(jnp.mean(feats * feats, axis=0, keepdims=True) + 1e-06)
    return feats, inv


def peer_of(k):
    return lax.axis_index("graph") ^ k


class Fetched:
    def __init__(self, source, held, sem):
        self.held = held
        self.copy = pltpu.make_async_copy(source, held, sem)
        self.copy.start()

    def take(self):
        if self.copy is not None:
            self.copy.wait()
            self.copy = None
        return self.held


class Many:
    def __init__(self, moves, held):
        self.held = held
        self.parts = [Fetched(*move) for move in moves]

    def take(self):
        for part in self.parts:
            part.take()
        return self.held


class Held:
    def __init__(self, held):
        self.held = held

    def take(self):
        return self.held


def with_fetches(kernel, kinds, ks, outs, *refs):
    refs = list(refs)
    count = sum(len(ks) if kind in ("many", "each") else 1 for kind in kinds)
    ins, refs = refs[:count], refs[count:]
    results, refs = refs[:outs], refs[outs:]
    given = []
    ins = iter(ins)
    for kind in kinds:
        ref = next(ins)
        if kind == "many":
            held, sems = refs.pop(0), refs.pop(0)
            sources = [ref] + [next(ins) for _ in ks[1:]]
            given.append(Many([(x, held.at[i], sems.at[i]) for i, x in enumerate(sources)], held))
        elif kind == "each":
            given.append(Held([ref] + [next(ins) for _ in ks[1:]]))
        elif kind == "edges":
            held, sems = refs.pop(0), refs.pop(0)
            given.append(Many([(ref.at[peer_of(k)], held.at[i], sems.at[i]) for i, k in enumerate(ks)], held))
        elif kind == "copy":
            given.append(Fetched(ref, refs.pop(0), refs.pop(0)))
        else:
            given.append(Held(ref))
    kernel(ks, *given, *results, *refs)


def back_table(w_out, cot, groups):
    back_t = (dot_nt(w_out[...], cot) * (1.0 / DEG_NORM)).astype(BF16)
    return stack_groups(back_t, groups)


def block_finder(ks, counts):
    sizes = [counts[lax.axis_index("graph"), peer_of(k)] for k in ks]
    firsts = [0]
    for size in sizes:
        firsts.append(firsts[-1] + (size + BLOCK - 1) // BLOCK)

    def locate(item):
        i = jnp.int32(0)
        first = jnp.int32(0)
        peer = peer_of(ks[0])
        size = sizes[0]
        for j in range(1, len(ks)):
            past = item >= firsts[j]
            i = jnp.where(past, j, i)
            first = jnp.where(past, firsts[j], first)
            peer = jnp.where(past, peer_of(ks[j]), peer)
            size = jnp.where(past, sizes[j], size)
        start = pl.multiple_of((item - first) * BLOCK, BLOCK)
        live = lax.broadcasted_iota(jnp.int32, (1, BLOCK), 1) + start < size
        return i, peer, pl.ds(start, BLOCK), live

    return firsts[-1], locate


def low_high(index, live):
    return jnp.where(live, index % GROUP, -1), index // GROUP


def edge_kernel(
    ks,
    atoms,
    gain,
    w_out,
    cots,
    w_src,
    w_edge,
    counts,
    src,
    dsts,
    edges,
    part_a,
    part_b,
    chunks,
    dpres,
    table,
    back,
    agg_sum,
    row_sum,
    edge_sum,
    hold,
):
    chans = edge_sum.shape[0]
    groups = back.shape[1] // chans
    agg_sum[...] = jnp.zeros_like(agg_sum)
    row_sum[...] = jnp.zeros_like(row_sum)
    edge_sum[...] = jnp.zeros_like(edge_sum)
    atoms, gain, w_out, cots = atoms.take(), gain.take(), w_out.take(), cots.take()
    cots = [cots[i][...] for i in range(len(ks))]
    w_src_t, w_edge_t = w_src.take()[...].T, w_edge.take()[...].T
    feats, inv = norm_parts(atoms[...])
    table[...] = stack_groups((feats * inv * column(gain)).astype(BF16), groups)
    for i in range(len(ks)):
        back[i] = back_table(w_out, cots[i], groups)
    counts, src, dsts, edges = counts.take(), src.take(), dsts.take(), edges.take()
    whole = edges.shape[0] != len(ks)
    me = lax.axis_index("graph")
    total, locate = block_finder(ks, counts)

    def gather(item):
        i, peer, span, live = locate(item)
        s_low, s_high = low_high(src[pl.ds(peer, 1), span], live)
        d_low, d_high = low_high(dsts[i, pl.ds(me, 1), span], live)
        rows = choose(dot(table[...], one_hot(s_low)), s_high, groups).astype(BF16)
        pre = dot(w_src_t, rows) + dot_nt(w_edge_t, edges[peer if whole else i, span, :])
        slot_back = choose(dot(back[i], one_hot(d_low)), d_high, groups)
        sig = 0.5 * jnp.tanh(0.5 * pre) + 0.5
        act = pre * sig
        slope = sig + act - act * sig
        return rows, act.astype(BF16), (slot_back * slope).astype(BF16)

    def add_up(item, rows, msg):
        i, peer, span, live = locate(item)
        d_low, d_high = low_high(dsts[i, pl.ds(me, 1), span], live)
        dpre = dpres[i, :, span]
        agg_sum[i] += dot_nt(spread(msg, d_high, groups), one_hot(d_low))
        edge_sum[...] += dot(dpre, edges[peer if whole else i, span, :])
        row_sum[...] += dot_nt(rows, dpre)

    def put(item, rows, msg, dpre):
        i, _, span, _ = locate(item)
        hold[0] = rows
        hold[1] = msg
        dpres[i, :, span] = dpre

    def step(item, carry):
        rows, msg = hold[0], hold[1]
        fresh = gather(item)
        add_up(item - 1, rows, msg)
        put(item, *fresh)
        return carry

    @pl.when(total > 0)
    def _():
        put(0, *gather(0))

    lax.fori_loop(1, total, step, 0)

    @pl.when(total > 0)
    def _():
        add_up(total - 1, hold[0], hold[1])

    grad_out = jnp.zeros((chans, chans), F32)
    for i in range(len(ks)):
        part = (unstack_groups(agg_sum[i], groups) * (1.0 / DEG_NORM)).astype(BF16)
        (part_a, part_b)[i][...] = part
        grad_out = grad_out + dot(part, cots[i])
    batches = chunks.shape[0]
    rows = chans // batches
    left = chunks.shape[1] - 3 * rows
    mine = lax.axis_index("dp")
    for n, grad in enumerate((row_sum[...], edge_sum[...].T, grad_out)):
        for j in range(batches):
            chunks[j ^ mine, n * rows : (n + 1) * rows, :] = grad[j * rows : (j + 1) * rows, :]
    if left:
        for j in range(batches):
            chunks[j, 3 * rows :, :] = jnp.zeros((left, chans), F32)


def source_kernel(ks, counts, src, dpres, *refs):
    *before, src_sum = refs
    groups = src_sum.shape[0] // dpres.held.shape[1]
    src_sum[...] = before[0].take()[...] if before else jnp.zeros_like(src_sum)
    counts, src, dpres = counts.take(), src.take(), dpres.take()
    total, locate = block_finder(ks, counts)

    def step(item, carry):
        i, peer, span, live = locate(item)
        s_low, s_high = low_high(src[pl.ds(peer, 1), span], live)
        src_sum[...] += dot_nt(spread(dpres[i, :, span], s_high, groups), one_hot(s_low))
        return carry

    lax.fori_loop(0, total, step, 0)


def atom_kernel(ks, atoms, gain, w_src, w_out, cot, src_sum, agg_a, agg_b, layer_out, grad_atoms):
    feats_rows = atoms.take()[...]
    feats, inv = norm_parts(feats_rows)
    groups = feats_rows.shape[0] // GROUP
    high, low = split(unstack_groups(src_sum.take()[...], groups))
    w_src = w_src.take()[...]
    scaled = column(gain.take()) * (dot(w_src, high) + dot(w_src, low))
    mean = jnp.mean(feats * scaled, axis=0, keepdims=True)
    rest = inv * scaled - feats * (inv * inv * inv * mean)
    grad_atoms[...] = (cot.take()[...].astype(F32) + rest.T).astype(BF16)
    agg = (agg_a.take()[...].astype(F32) + agg_b.take()[...].astype(F32)).T.astype(BF16)
    layer_out[...] = (feats_rows.astype(F32) + dot(agg, w_out.take()[...])).astype(BF16)


def weight_kernel(ks, ours, theirs, w_src, gain, grad_src, grad_edge, grad_out, grad_gain):
    rows, chans = grad_src.shape
    total = ours.take()[...] + theirs.take()[...]
    for n, out in enumerate((grad_src, grad_edge, grad_out)):
        out[...] = total[n * rows : (n + 1) * rows, :]
    place = lax.broadcasted_iota(jnp.int32, (rows, chans), 1)
    row = lax.broadcasted_iota(jnp.int32, (rows, chans), 0)
    mine = place == row + lax.axis_index("dp") * rows
    w_rows = dot(jnp.where(mine, 1.0, 0.0).astype(BF16), w_src.take()[...])
    gains = jnp.sum(jnp.where(mine, gain.take()[...], 0.0), axis=1, keepdims=True)
    value = jnp.sum(w_rows * total[:rows, :], axis=1, keepdims=True) / gains
    grad_gain[...] = jnp.sum(jnp.where(place == row, value, 0.0), axis=0, keepdims=True)[:, :rows]


def move(x, axis, bit):
    size = lax.axis_size(axis)
    return lax.ppermute(x, axis, [(i, i ^ bit) for i in range(size)])


def reduce_batches(chunks, bits):
    for _ in range(bits):
        batches, rows, width = chunks.shape
        bit = lax.axis_size("dp") // batches
        pair = chunks.reshape(batches // 2, 2, rows, width)
        chunks = pair[:, 0] + move(pair[:, 1].astype(BF16), "dp", bit).astype(F32)
    return chunks


def body(atoms, gain, w_src, w_edge, w_out, send_src, recv_dst, edge_count, edge_feat, cotangent):
    shards = lax.axis_size("graph")
    batches = lax.axis_size("dp")
    atom_count, chans = atoms.shape[2:]
    slots = send_src.shape[3]
    groups = atom_count // GROUP
    feats = atoms.reshape(atom_count, chans)
    src = send_src.reshape(shards, slots)
    dst_here = recv_dst.reshape(shards, slots)
    cot = cotangent.reshape(atom_count, chans)
    gain_row = gain.reshape(1, chans)
    edges = edge_feat.reshape(shards, slots, edge_feat.shape[4])
    counts = edge_count.reshape(shards, shards)

    far_dst = move(dst_here, "graph", 2)
    far = move(cot, "graph", 2)
    dst = [dst_here, move(dst_here, "graph", 1)]
    cots = [cot, move(cot, "graph", 1), far]

    vmem = pl.BlockSpec(memory_space=pltpu.VMEM)
    hbm = pl.BlockSpec(memory_space=pltpu.HBM)

    def call(kernel, ks, outs, ins, scratch, name, flops, limit, fetch=False):
        kinds, flat, buffers, here = [], [], [], set()
        for x in ins:
            if isinstance(x, list) and not fetch and x[0].dtype == BF16:
                kinds.append("each")
                flat += x
                here.update(id(y) for y in x)
            elif isinstance(x, list):
                kinds.append("many")
                flat += x
                buffers += [pltpu.VMEM((len(x),) + x[0].shape, x[0].dtype), pltpu.SemaphoreType.DMA((len(x),))]
            elif x is edges and fetch:
                kinds.append("edges")
                flat.append(x)
                buffers += [pltpu.VMEM((len(ks),) + x.shape[1:], x.dtype), pltpu.SemaphoreType.DMA((len(ks),))]
            elif x is not counts and not fetch:
                kinds.append("here")
                flat.append(x)
                here.add(id(x))
            else:
                kinds.append("copy")
                flat.append(x)
                space = pltpu.SMEM if x is counts else pltpu.VMEM
                buffers += [space(x.shape, x.dtype), pltpu.SemaphoreType.DMA]
        return pl.pallas_call(
            functools.partial(with_fetches, kernel, kinds, ks, len(outs)),
            out_shape=tuple(jax.ShapeDtypeStruct(shape, kind) for shape, kind in outs),
            in_specs=[vmem if id(x) in here else hbm for x in flat],
            out_specs=(vmem,) * len(outs),
            scratch_shapes=buffers + scratch,
            compiler_params=pltpu.CompilerParams(vmem_limit_bytes=limit),
            cost_estimate=pl.CostEstimate(flops=flops, bytes_accessed=min(flops, 1 << 20), transcendentals=0),
            name=name,
        )(*flat)

    tall = (groups * chans, GROUP)
    part_shape = (chans, atom_count)
    unit = 2 * slots * atom_count * chans

    def work(ks):
        return [
            pltpu.VMEM(tall, BF16),
            pltpu.VMEM((len(ks),) + tall, BF16),
            pltpu.VMEM((len(ks),) + tall, F32),
            pltpu.VMEM((chans, chans), F32),
            pltpu.VMEM((chans, chans), F32),
            pltpu.VMEM((2, chans, BLOCK), BF16),
        ]

    near, distant = (0, 1), (2, 3)
    rows = chans // batches
    chunk_rows = -(-3 * rows // 8) * 8
    outs = [
        (part_shape, BF16),
        (part_shape, BF16),
        ((batches, chunk_rows, chans), F32),
        ((2, chans, slots), BF16),
    ]
    *near_parts, near_chunks, near_dpre = call(
        edge_kernel,
        near,
        outs,
        [feats, gain_row, w_out, cots[:2], w_src, w_edge, counts, src, dst[:2], edges],
        work(near),
        "near_edges",
        1,
        NEAR_VMEM_BYTES,
        fetch=True,
    )
    far, far_dst, near_chunks = lax.optimization_barrier((far, far_dst, near_chunks))
    dst = dst + [far_dst, move(far_dst, "graph", 1)]
    cots = cots[:2] + [far, move(far, "graph", 1)]
    *far_parts, far_chunks, far_dpre = call(
        edge_kernel,
        distant,
        outs,
        [feats, gain_row, w_out, cots[2:], w_src, w_edge, counts, src, dst[2:], edges],
        work(distant),
        "far_edges",
        8 * unit,
        FAR_VMEM_BYTES,
    )
    chunks = near_chunks + far_chunks

    def sum_sources(ks, dpre, before, name):
        (total,) = call(
            source_kernel,
            ks,
            [(tall, F32)],
            [counts, src, dpre] + before,
            [],
            name,
            unit,
            FAR_VMEM_BYTES,
        )
        return total

    given_far = move(far_parts[1], "graph", 1)
    src_sum = sum_sources(near, near_dpre, [], "near_sources")
    given_far, src_sum = lax.optimization_barrier((given_far, src_sum))
    far_part = (far_parts[0].astype(F32) + given_far.astype(F32)).astype(BF16)
    arrived = move(far_part, "graph", 2)
    own_part = near_parts[0].astype(F32) + move(near_parts[1], "graph", 1).astype(F32)
    chunks = reduce_batches(chunks, 1)
    chunks, src_sum, far_dpre = lax.optimization_barrier((chunks, src_sum, far_dpre))
    src_sum = sum_sources(distant, far_dpre, [src_sum], "far_sources")
    chunks = reduce_batches(chunks, 1)
    chunks, src_sum = lax.optimization_barrier((chunks, src_sum))
    chunks = reduce_batches(chunks, batches.bit_length() - 3)
    chunks, arrived = lax.optimization_barrier((chunks, arrived))
    total = chunks.reshape(chunk_rows, chans)
    total = total + move(total, "graph", 2)

    layer_out, grad_atoms = call(
        atom_kernel,
        (),
        [(feats.shape, BF16)] * 2,
        [feats, gain_row, w_src, w_out, cot, src_sum, own_part, arrived],
        [],
        "atoms",
        unit // 8,
        FAR_VMEM_BYTES,
    )

    total, layer_out, grad_atoms = lax.optimization_barrier((total, layer_out, grad_atoms))
    theirs = move(total, "graph", 1)
    grads = call(
        weight_kernel,
        (),
        [((rows, chans), F32)] * 3 + [((1, rows), F32)],
        [total, theirs, w_src, gain_row],
        [],
        "weights",
        1,
        FAR_VMEM_BYTES,
    )
    return (
        layer_out.reshape(atoms.shape),
        grad_atoms.reshape(atoms.shape),
        *grads[:3],
        grads[3].reshape(rows),
    )


def solution(mesh):
    in_specs = (
        P("dp", "graph", None, None),
        P(),
        P(),
        P(),
        P(),
        P("dp", "graph", None, None),
        P("dp", "graph", None, None),
        P("dp", None, None),
        P("dp", "graph", None, None, None),
        P("dp", "graph", None, None),
    )
    out_specs = (
        P("dp", "graph", None, None),
        P("dp", "graph", None, None),
        P("dp", None),
        P("dp", None),
        P("dp", None),
        P("dp"),
    )
    return jax.shard_map(body, mesh=mesh, in_specs=in_specs, out_specs=out_specs, check_vma=False)
```
